256 devices in a mesh: face: 4 (over x), tile: 16 (over z, core), dp: 4 (over y).
Axes of the slice: x: 4, y: 4, z: 8, core: 2. Of those that a mesh axis runs over, the one named last changes fastest.
Arguments:
- inputs: bfloat16 [4, 384, 90, 2880], P('dp', ('face', 'tile')), may hold values from -6 to 6
- cotangent: bfloat16 [4, 384, 90, 2880], P('dp', ('face', 'tile')), may hold values from -6 to 6
- conv_weight: bfloat16 [288, 32], replicated, may hold values from -0.375 to 0.375
- out_bias: float32 [32], replicated, may hold values from -3 to 3
- cell_area: float32 [384, 8100], P(('face', 'tile')), may hold values from 0.25 to 4
- land_mask: int32 [384, 8100], P(('face', 'tile')), may hold values 0 or 1
- neighbours: int32 [384, 4], P(('face', 'tile')), may hold values from -1 to 383, as said below
- reversal: int32 [384, 4], P(('face', 'tile')), may hold values from 0 to 1, as said below
- wet_count: int32 [64], P(('face', 'tile')), may hold values from 1 to 6, as said below
Outputs:
- outputs: bfloat16 [4, 384, 90, 2880], P('dp', ('face', 'tile'))
- input_grad: bfloat16 [4, 384, 90, 2880], P('dp', ('face', 'tile'))
- weight_grad: float32 [288, 32], replicated
- bias_grad: float32 [32], replicated
The draws below stay inside these ranges and needn't reach their ends.
Inputs may be any that keep to these rules, and one draw needn't show every extreme that they name: Device group g = face index * 16 + tile index holds slots g * 6 to g * 6 + 5. Entry [s, 0] is -1 or a slot of the group one step up along tile (wrapping), [s, 1] one step down along tile, [s, 2] one step up along face (wrapping), [s, 3] one step down along face. No entry names a slot at or past its group's wet_count, and a slot past its own group's wet_count has only -1. If neighbours[s, d] = m >= 0 then neighbours[m, (1, 0, 3, 2)[d]] = s. `reversal`: zero where neighbours is -1; equal on the two sides of each seam. `wet_count`: wet tiles of a group fill its slots from position 0; some group holds 6.
All inputs are finite; a program needn't handle non-finite values. No bound on the sum of `land_mask` on one device may be relied on, other than what follows from the above.
Results may differ from the reference program's by a relative error of at most 0.0049.
Values may be sent and summed in bfloat16 or wider, within the bound.
A program may use at most 192 MiB of HBM per device.

```python
import math
import jax
import jax.numpy as jnp
from jax import lax

TILE = 90
CH = 32
TILES_DEV = 6
SLOTS = 384
BATCH = 4
N_FACE = 4
N_TILE = 16


def topology(key):
    groups = N_FACE * N_TILE
    key_list = jax.random.split(key, 5)
    full_group = jax.random.randint(key_list[0], (), 0, groups)
    counts = jax.random.randint(key_list[1], (groups,), (TILES_DEV + 1) // 2, TILES_DEV + 1)
    counts = counts.at[full_group].set(TILES_DEV)
    position = jnp.arange(TILES_DEV, dtype=jnp.int32)
    occupied = position[None, :] < counts[:, None]
    perm_keys = jax.random.split(key_list[2], 2 * groups)
    orders = jax.vmap(lambda subkey: jax.random.permutation(subkey, TILES_DEV))(perm_keys).reshape(2, groups, TILES_DEV)
    kept_link = jax.random.randint(key_list[3], (2, groups, TILES_DEV), 0, 8) > 0
    flip_bits = jax.random.randint(key_list[4], (2, groups, TILES_DEV), 0, 2)
    group_ids = jnp.arange(groups, dtype=jnp.int32)
    face_of = group_ids // N_TILE
    tile_of = group_ids % N_TILE
    upward = [face_of * N_TILE + (tile_of + 1) % N_TILE, (face_of + 1) % N_FACE * N_TILE + tile_of]
    own_slot = group_ids[:, None] * TILES_DEV + position[None, :]
    side_lists = []
    flip_lists = []
    for axis_pick in range(2):
        target = upward[axis_pick]
        partner_pos = orders[axis_pick].astype(jnp.int32)
        linked = occupied & occupied[target[:, None], partner_pos] & kept_link[axis_pick]
        low_side = jnp.where(linked, target[:, None] * TILES_DEV + partner_pos, -1)
        high_side = jnp.full((groups, TILES_DEV), -1, jnp.int32).at[target[:, None], partner_pos].set(jnp.where(linked, own_slot, -1))
        low_flip = jnp.where(linked, flip_bits[axis_pick], 0)
        high_flip = jnp.zeros((groups, TILES_DEV), jnp.int32).at[target[:, None], partner_pos].set(low_flip)
        side_lists = side_lists + [low_side, high_side]
        flip_lists = flip_lists + [low_flip, high_flip]
    neighbours = jnp.stack(side_lists, -1).reshape(groups * TILES_DEV, 4).astype(jnp.int32)
    reversal = jnp.stack(flip_lists, -1).reshape(groups * TILES_DEV, 4).astype(jnp.int32)
    return (neighbours, reversal, counts.astype(jnp.int32))


def draw_neighbours(key, part):
    return topology(key)[0]


def draw_reversal(key, part):
    return topology(key)[1]


def draw_wet_count(key, part):
    return topology(key)[2]


def with_ends(values, stream_key, low, largest):
    spot = [jax.random.randint(jax.random.fold_in(stream_key, axis), (), 0, length) for axis, length in enumerate(values.shape)]
    main_axis = values.shape.index(max(values.shape))
    beside = spot[:main_axis] + [(spot[main_axis] + 1) % values.shape[main_axis]] + spot[main_axis + 1:]
    return values.at[tuple(spot)].set(low).at[tuple(beside)].set(largest)


def block_scale(rng, dims, cuts, least, top_value):
    loudness, own = 1.0, jax.random.fold_in(rng, 6)
    for axis_at, blocks in cuts:
        steps = jnp.exp(jax.random.uniform(jax.random.fold_in(own, axis_at), (blocks,), jnp.float32, least / len(cuts), top_value / len(cuts)))
        loudness = loudness * jnp.repeat(steps, dims[axis_at] // blocks).reshape([-1 if axis == axis_at else 1 for axis in range(len(dims))])
    return loudness


def gaussian(own_key, extent, scale, limit, shards=(), kind=jnp.bfloat16):
    values = scale * jax.random.normal(own_key, extent, jnp.float32)
    if shards:
        values = values * block_scale(own_key, extent, shards, -0.22, 0.18)
    return jnp.clip(values, -limit, limit).astype(kind)


def setup_inputs(seed: int = 0) -> dict:
    streams_of = jax.random.split(jax.random.key(seed), 10)
    inputs = gaussian(streams_of[0], (BATCH, SLOTS, TILE, TILE * CH), 1.0, 6.0, ((0, 4), (1, 64)))
    cotangent = gaussian(streams_of[1], (BATCH, SLOTS, TILE, TILE * CH), 1.0, 6.0, ((0, 4), (1, 64)))
    conv_weight = gaussian(streams_of[2], (9 * CH, CH), (9 * CH) ** -0.5, 0.375)
    out_bias = gaussian(streams_of[3], (CH,), 0.5, 3.0, (), jnp.float32)
    cell_area = jnp.clip(jnp.exp(math.log(4.0) - 2.7725887 * jax.random.uniform(streams_of[4], (SLOTS, TILE * TILE), jnp.float32) ** block_scale(streams_of[4], (SLOTS, TILE * TILE), ((0, 64),), -0.2, 0.2)), 0.25, 4.0)
    land_mask = with_ends((jax.random.randint(streams_of[5], (SLOTS, TILE * TILE), 0, 8) < 7).astype(jnp.int32), jax.random.fold_in(streams_of[5], 1), 0, 1)
    neighbours = draw_neighbours(jax.random.fold_in(streams_of[9], 71), 0)
    reversal = draw_reversal(jax.random.fold_in(streams_of[9], 71), 0)
    wet_count = draw_wet_count(jax.random.fold_in(streams_of[9], 71), 0)
    return {"inputs": inputs, "cotangent": cotangent, "conv_weight": conv_weight, "out_bias": out_bias, "cell_area": cell_area, "land_mask": land_mask, "neighbours": neighbours, "reversal": reversal, "wet_count": wet_count}


PARTNER = (1, 0, 3, 2)

def route(pieces, neighbours, reversal):
    partner_slot = jnp.maximum(neighbours, 0)
    fetched = pieces[:, partner_slot, jnp.array(PARTNER, dtype=jnp.int32)[None, :]]
    flipped = fetched[:, :, :, ::-1]
    chosen = jnp.where((reversal == 1)[None, :, :, None, None], flipped, fetched)
    return jnp.where((neighbours >= 0)[None, :, :, None, None], chosen, jnp.zeros_like(chosen))

def unfold(padded_tile):
    parts = []
    for row_off in range(3):
        for col_off in range(3):
            parts.append(padded_tile[:, row_off:row_off + TILE, col_off:col_off + TILE])
    return jnp.concatenate(parts, -1).reshape(-1, 9 * CH)

def kernel_part(conv_weight, row_off, col_off):
    start = (3 * row_off + col_off) * CH
    return conv_weight[start:start + CH].astype(jnp.float32)

def rim_line(rim_cells, parts):
    padded_line = jnp.pad(rim_cells.astype(jnp.float32), ((0, 0), (0, 0), (1, 1), (0, 0)))
    summed = jnp.zeros(rim_cells.shape, jnp.float32)
    for offset in range(3):
        window = padded_line[:, :, 2 - offset:2 - offset + TILE]
        summed = summed + jnp.einsum('bsto,io->bsti', window, parts[offset])
    return summed.astype(jnp.bfloat16)

def reference(inputs, cotangent, conv_weight, out_bias, cell_area, land_mask, neighbours, reversal, wet_count):
    slot_ids = jnp.arange(SLOTS, dtype=jnp.int32)
    owner_group = slot_ids // TILES_DEV
    occupied = (slot_ids % TILES_DEV < wet_count[owner_group]).astype(jnp.float32)
    wet_cells = land_mask.reshape(SLOTS, TILE, TILE).astype(jnp.float32) * occupied[:, None, None]
    tiles_in = inputs.reshape(BATCH, SLOTS, TILE, TILE, CH)
    masked = (tiles_in.astype(jnp.float32) * wet_cells[None, :, :, :, None]).astype(jnp.bfloat16)
    edges = jnp.stack([masked[:, :, 0], masked[:, :, TILE - 1], masked[:, :, :, TILE - 1], masked[:, :, :, 0]], 2)
    strips = route(edges, neighbours, reversal)
    padded = jnp.pad(masked, ((0, 0), (0, 0), (1, 1), (1, 1), (0, 0)))
    padded = padded.at[:, :, 0, 1:-1].set(strips[:, :, 0])
    padded = padded.at[:, :, TILE + 1, 1:-1].set(strips[:, :, 1])
    padded = padded.at[:, :, 1:-1, TILE + 1].set(strips[:, :, 2])
    padded = padded.at[:, :, 1:-1, 0].set(strips[:, :, 3])
    area_cells = cell_area.reshape(SLOTS, TILE, TILE)
    scaled = (wet_cells[None, :, :, :, None] * area_cells[None, :, :, :, None] * cotangent.reshape(BATCH, SLOTS, TILE, TILE, CH).astype(jnp.float32)).astype(jnp.bfloat16)

    def forward_tile(packed):
        padded_tile, scaled_tile, wet_tile = packed
        patches = unfold(padded_tile)
        result = jnp.dot(patches, conv_weight, preferred_element_type=jnp.float32) + out_bias
        produced = (wet_tile[None, :, :, None] * result.reshape(BATCH, TILE, TILE, CH)).astype(jnp.bfloat16)
        flat_grad = scaled_tile.reshape(-1, CH)
        weight_acc = lax.dot_general(patches, flat_grad, (((0,), (0,)), ((), ())), preferred_element_type=jnp.float32)
        bias_acc = lax.optimization_barrier(jnp.sum(flat_grad.astype(jnp.float32), 0))
        return (produced, weight_acc, bias_acc)
    produced, weight_acc, bias_acc = lax.map(forward_tile, (jnp.moveaxis(padded, 1, 0), jnp.moveaxis(scaled, 1, 0), wet_cells))
    cell_norm = math.sqrt(BATCH * SLOTS * TILE * TILE)
    weight_grad = lax.optimization_barrier(jnp.sum(weight_acc, 0)) / cell_norm
    bias_grad = lax.optimization_barrier(jnp.sum(bias_acc, 0)) / cell_norm
    outputs = jnp.moveaxis(produced, 0, 1).reshape(BATCH, SLOTS, TILE, TILE * CH)
    rim_grad = jnp.stack([rim_line(scaled[:, :, 0], [kernel_part(conv_weight, 0, col) for col in range(3)]), rim_line(scaled[:, :, TILE - 1], [kernel_part(conv_weight, 2, col) for col in range(3)]), rim_line(scaled[:, :, :, TILE - 1], [kernel_part(conv_weight, row, 2) for row in range(3)]), rim_line(scaled[:, :, :, 0], [kernel_part(conv_weight, row, 0) for row in range(3)])], 2)
    returned = route(rim_grad, neighbours, reversal)

    def backward_tile(packed):
        scaled_tile, returned_tile, wet_tile = packed
        flat_grad = scaled_tile.reshape(-1, CH)
        patch_grad = lax.dot_general(flat_grad, conv_weight, (((1,), (1,)), ((), ())), preferred_element_type=jnp.float32)
        pad_grad = jnp.zeros((BATCH, TILE + 2, TILE + 2, CH), jnp.float32)
        for row_off in range(3):
            for col_off in range(3):
                start = (3 * row_off + col_off) * CH
                piece = patch_grad[:, start:start + CH].reshape(BATCH, TILE, TILE, CH)
                pad_grad = pad_grad.at[:, row_off:row_off + TILE, col_off:col_off + TILE].add(piece)
        interior = pad_grad[:, 1:-1, 1:-1]
        interior = interior.at[:, 0].add(returned_tile[:, 0].astype(jnp.float32))
        interior = interior.at[:, TILE - 1].add(returned_tile[:, 1].astype(jnp.float32))
        interior = interior.at[:, :, TILE - 1].add(returned_tile[:, 2].astype(jnp.float32))
        interior = interior.at[:, :, 0].add(returned_tile[:, 3].astype(jnp.float32))
        return (wet_tile[None, :, :, None] * interior).astype(jnp.bfloat16)
    grads = lax.map(backward_tile, (jnp.moveaxis(scaled, 1, 0), jnp.moveaxis(returned, 1, 0), wet_cells))
    input_grad = jnp.moveaxis(grads, 0, 1).reshape(BATCH, SLOTS, TILE, TILE * CH)
    return (outputs, input_grad, weight_grad, bias_grad)
```

```python
import functools
import math

import jax
import jax.numpy as jnp
import ml_dtypes
import numpy as np
from jax import lax
from jax.experimental import pallas as pl
from jax.experimental.pallas import tpu as pltpu
from jax.sharding import PartitionSpec as P

MESH = pl.DeviceIdType.MESH
BF = jnp.bfloat16
F32 = jnp.float32
T = 90
C = 32
SL = 6
G = 96
R = SL * G
W = T * C
WP = 3072
NB = 12
LAST = W - 11 * 256
VMEM_LIMIT = 62 * 2**20


def spread_matrix():
    m = np.zeros((256, WP), np.float32)
    for j in range(T):
        m[j, j * C : (j + 1) * C] = 1
        m[128 + j, j * C : (j + 1) * C] = 1
    return m.astype(ml_dtypes.bfloat16)


def flip_lanes_matrix():
    m = np.zeros((256, 128), np.float32)
    for q in range(4):
        for k in range(C):
            m[C * (5 - q) + k, C * q + k] = 1
    return m.astype(ml_dtypes.bfloat16)


def flip_rows_matrix():
    m = np.zeros((G, G), np.float32)
    for i in range(T):
        m[i, T - 1 - i] = 1
    return m.astype(ml_dtypes.bfloat16)


def dot(a, b):
    return jnp.dot(a, b, preferred_element_type=F32)


def dot_t(a, b):
    return lax.dot_general(a, b, (((1,), (1,)), ((), ())), preferred_element_type=F32)


def split_hi_lo(v):
    hi = v.astype(BF)
    lo = (v - hi.astype(F32)).astype(BF)
    return hi, lo


def edge_kernel(
    xr0, xr1, xc0, xc1, gr0, gr1, gc0, gc1, wa, spread, r0_out, r1_out, c0_out, c1_out
):
    def rows_of(ref, row):
        parts = [ref[0, s, row : row + 1, :].astype(F32) for s in range(SL)]
        v = jnp.concatenate(parts + [jnp.zeros((2, W), F32)], 0)
        return jnp.concatenate([v, jnp.zeros((8, WP - W), F32)], 1)

    area = jnp.concatenate(
        [wa[s, 0:1, :] for s in range(SL)]
        + [jnp.zeros((2, T), F32)]
        + [wa[s, T - 1 : T, :] for s in range(SL)]
        + [jnp.zeros((2, T), F32)],
        0,
    )
    area = jnp.concatenate([area, jnp.zeros((16, 128 - T), F32)], 1)
    hi, lo = split_hi_lo(area)
    wide = dot(jnp.concatenate([hi, lo], 1), spread[...])
    for row, x_ref, g_ref, e, out in (
        (0, xr0, gr0, wide[0:8], r0_out),
        (T - 1 - 80, xr1, gr1, wide[8:16], r1_out),
    ):
        xv = jnp.where(e > 0, rows_of(x_ref, row), 0.0)
        gv = jnp.where(e > 0, e * rows_of(g_ref, row), 0.0)
        out[...] = jnp.concatenate([xv, gv], 0).astype(BF)
    pad = jnp.zeros((G - T, 128), BF)
    for lane, col, x_ref, g_ref, out in ((0, 0, xc0, gc0, c0_out), (C, T - 1, xc1, gc1, c1_out)):
        for s in range(SL):
            e = jnp.broadcast_to(wa[s, :, col : col + 1], (T, C))
            xv = jnp.where(e > 0, x_ref[0, s, :, lane : lane + C].astype(F32), 0.0)
            gv = jnp.where(e > 0, e * g_ref[0, s, :, lane : lane + C].astype(F32), 0.0)
            v = jnp.concatenate([xv, gv, jnp.zeros((T, 64), F32)], 1).astype(BF)
            out[s * G : (s + 1) * G] = jnp.concatenate([v, pad], 0)


def edges(x, g, wa, spread):
    row_lo = pl.BlockSpec((1, SL, 16, W), lambda i: (0, 0, 0, 0))
    row_hi = pl.BlockSpec((1, SL, 16, W), lambda i: (0, 0, 5, 0))
    col_lo = pl.BlockSpec((1, SL, T, 128), lambda i: (0, 0, 0, 0))
    col_hi = pl.BlockSpec((1, SL, T, 128), lambda i: (0, 0, 0, 22))

    def whole(shape):
        return pl.BlockSpec(shape, lambda i: (0,) * len(shape))

    return pl.pallas_call(
        edge_kernel,
        grid=(1,),
        in_specs=[row_lo, row_hi, col_lo, col_hi] * 2
        + [whole((SL, T, T)), whole((256, WP))],
        out_specs=[whole((16, WP))] * 2 + [whole((R, 128))] * 2,
        out_shape=[jax.ShapeDtypeStruct((16, WP), BF)] * 2
        + [jax.ShapeDtypeStruct((R, 128), BF)] * 2,
        compiler_params=pltpu.CompilerParams(vmem_limit_bytes=40 * 2**20),
    )(x, x, x, x, g, g, g, g, wa, spread)


def main_kernel(
    nb,
    rev,
    x_hbm,
    g_hbm,
    wa,
    spread,
    flip_l,
    flip_r,
    weight,
    bias,
    ra,
    rb,
    ca,
    cb,
    y_hbm,
    gi_hbm,
    part_out,
    xs,
    gs,
    x3,
    s3,
    xp,
    qx,
    qs,
    wet,
    cols,
    in_sem,
    out_sem,
):
    yo, go = xs, gs
    copies = []
    for s in range(SL):
        copies.append(pltpu.make_async_copy(x_hbm.at[0, s], xs.at[s], in_sem.at[0, s]))
        copies.append(pltpu.make_async_copy(g_hbm.at[0, s], gs.at[s], in_sem.at[1, s]))
    for copy in copies:
        copy.start()

    w = weight[...].astype(F32)

    def tap(a, c):
        start = (3 * a + c) * C
        return w[start : start + C]

    def band(a, cells_in, shift, mirror=False):
        rows_iota = lax.broadcasted_iota(jnp.int32, (256, cells_in * C), 0) // C
        lanes_iota = lax.broadcasted_iota(jnp.int32, (256, cells_in * C), 1) // C - shift
        which = rows_iota - lanes_iota + 1
        if mirror:
            which = 2 - which
        out = jnp.zeros((256, cells_in * C), F32)
        for c in range(3):
            wide = jnp.concatenate([tap(a, c)] * 4, 1)
            wide = jnp.concatenate([wide] * (cells_in // 4), 1)
            out = jnp.where(which == c, jnp.concatenate([wide] * 8, 0), out)
        return out.astype(BF)

    bands = [band(a, 8, 0) for a in range(3)]
    z32 = jnp.zeros((C, C), F32)
    z64 = jnp.zeros((C, 192), F32)
    wq_rows = []
    for slot in (0, None, 1, 2):
        if slot is None:
            continue
        wq_rows.append(jnp.concatenate([tap(slot, 0), z32, z64], 1))
        wq_rows.append(jnp.concatenate([z64, z32, tap(slot, 2)], 1))
    wq = jnp.concatenate(wq_rows + [jnp.zeros((64, 256), F32)], 0).astype(BF)
    gl = jnp.concatenate(
        [v for a in range(3) for v in (tap(2 - a, 2), z32)] + [z32, z32], 1
    )
    gr = jnp.concatenate(
        [v for a in range(3) for v in (z32, tap(2 - a, 0))] + [z32, z32], 1
    )
    wqb = jnp.concatenate([gl, jnp.zeros((192, 256), F32), gr], 0).astype(BF)

    zr = jnp.concatenate([ra[...], rb[...]], 0)
    zpad = jnp.concatenate([jnp.zeros((32, 128), BF), zr], 1)
    stacked = jnp.concatenate(
        [zpad[:, 128 * (22 - n) : 128 * (24 - n)] for n in range(23)], 0
    )
    turned = dot(stacked, flip_l[...]).astype(BF)
    flipped = jnp.concatenate(
        [turned[32 * n : 32 * n + 32] for n in range(23)] + [jnp.zeros((32, 128), BF)], 1
    )
    lane_i = lax.broadcasted_iota(jnp.int32, (128, 64), 1)
    row_i = lax.broadcasted_iota(jnp.int32, (128, 64), 0)
    sel = jnp.zeros((128, 64), F32)
    for s in range(SL):
        for side, halo_row in ((0, (16 * (s - 1) + 15) % 96), (1, 16 * s + 10)):
            n, r = nb[s, side], rev[s, side]
            src = 16 * side + 32 * r + lax.rem(jnp.maximum(n, 0), SL)
            src = jnp.where(n >= 0, src, -100)
            sel = jnp.where((row_i == halo_row) & (lane_i == src), 1.0, sel)
            rim_row = 96 + 16 * side + 8 * r + s
            sel = jnp.where((row_i == rim_row) & (lane_i == src + 8), 1.0, sel)
    routed = dot(sel.astype(BF), jnp.concatenate([zr, flipped], 0))
    hx = routed[0:96]
    hs = routed[96:128].astype(BF)
    hs = jnp.concatenate(
        [jnp.zeros((32, 128), BF), hs, jnp.zeros((32, 128), BF)], 1
    )
    rim = []
    for side, a in ((0, 2), (1, 0)):
        total = None
        for r in range(2):
            rows = hs[16 * side + 8 * r : 16 * side + 8 * r + 8].astype(F32)
            lhs = jnp.concatenate(
                [rows[:, 256 * m : 256 * m + 512] for m in range(NB)], 0
            ).astype(BF)
            part = dot_t(lhs, band(a, 16, 4, mirror=(r == 1)))
            total = part if total is None else total + part
        rim.append(total.astype(BF).astype(F32))

    for side, ref in ((0, ca), (1, cb)):
        flat = jnp.concatenate([ref[s * G : (s + 1) * G] for s in range(SL)], 1)
        back = dot(flip_r[...], flat)
        for s in range(SL):
            cols[side, 0, s] = ref[s * G : (s + 1) * G].astype(F32)
            cols[side, 1, s] = back[:, 128 * s : 128 * s + 128]
    ecol, xleft, xright = [], [], []
    for s in range(SL):
        got = []
        pieces = []
        for side in range(2):
            n, r = nb[s, 2 + side], rev[s, 2 + side]
            v = cols[side, r, lax.rem(jnp.maximum(n, 0), SL)]
            v = jnp.where(n >= 0, v, 0.0)
            got.append(v)
            pieces.append(jnp.where(r == 0, v, 0.0)[:, C : 2 * C])
            pieces.append(jnp.where(r == 1, v, 0.0)[:, C : 2 * C])
        ecol.append(jnp.concatenate(pieces, 1))
        xright.append(got[0])
        xleft.append(got[1])
    ecol = jnp.concatenate(ecol, 0)
    xright = jnp.concatenate(xright, 0)
    xleft = jnp.concatenate(xleft, 0)
    e3 = jnp.concatenate(
        [pltpu.roll(ecol, 1, 0), ecol, pltpu.roll(ecol, R - 1, 0)], 1
    ).astype(BF)
    v2 = jnp.concatenate(
        [v for a in range(3) for v in (tap(2 - a, 0), tap(a, 0), z32, z32)], 1
    )
    v3 = jnp.concatenate(
        [v for a in range(3) for v in (z32, z32, tap(2 - a, 2), tap(a, 2))], 1
    )
    rim_col = dot_t(e3, jnp.concatenate([v2, v3], 0).astype(BF)).astype(BF).astype(F32)
    zc = jnp.zeros((R, C), F32)
    z6 = jnp.zeros((R, 192), F32)
    rim_first = jnp.concatenate([rim_col[:, C : 2 * C], zc, z6], 1)
    rim_last = jnp.concatenate([zc, rim_col[:, 0:C], z6], 1)
    halo_right = jnp.concatenate([zc, zc, xright[:, 0:C], jnp.zeros((R, 160), F32)], 1)
    xleft = xleft[:, 0:C].astype(BF)

    area = []
    for s in range(SL):
        v = jnp.concatenate([wa[s], jnp.zeros((G - T, T), F32)], 0)
        area.append(jnp.concatenate([v, jnp.zeros((G, 128 - T), F32)], 1))
    hi, lo = split_hi_lo(jnp.concatenate(area, 0))
    area = jnp.concatenate([hi, lo], 1)

    for copy in copies:
        copy.wait()

    def fetch(ref, m):
        parts = []
        for s in range(SL):
            lanes = LAST if m == NB - 1 else 256
            v = ref[s, :, 256 * m : 256 * m + lanes].astype(F32)
            if lanes < 256:
                v = jnp.concatenate([v, jnp.zeros((T, 256 - lanes), F32)], 1)
            parts.append(v)
            parts.append(jnp.zeros((G - T, 256), F32))
        return jnp.concatenate(parts, 0)

    def down(v):
        return jnp.concatenate([v[R - 1 :], v[: R - 1]], 0)

    def up(v):
        return jnp.concatenate([v[1:], v[:1]], 0)

    bias_acc = jnp.zeros((8, 256), F32)
    for m in range(NB):
        blk = slice(256 * m, 256 * m + 256)
        e = dot(area, spread[:, blk])
        wet[:, blk] = (e > 0).astype(F32).astype(BF)
        xv = jnp.where(e > 0, fetch(xs, m), 0.0)
        parts = []
        for s in range(SL):
            parts.append(xv[G * s : G * s + 80])
            parts.append(xv[G * s + 80 : G * s + 96] + hx[16 * s : 16 * s + 16, blk])
        xv = jnp.concatenate(parts, 0)
        if m == NB - 1:
            xv = xv + halo_right
        xv = xv.astype(BF)
        x3[0, :, blk] = down(xv)
        x3[1, :, blk] = xv
        x3[2, :, blk] = up(xv)
        sv = jnp.where(e > 0, e * fetch(gs, m), 0.0).astype(BF)
        s3[0, :, blk] = down(sv)
        s3[1, :, blk] = sv
        s3[2, :, blk] = up(sv)
        bias_acc = bias_acc + jnp.sum(sv.astype(F32).reshape(R // 8, 8, 256), 0)

    zb = jnp.zeros((R, C), BF)
    lane128 = lax.broadcasted_iota(jnp.int32, (R, 128), 1)
    for m in range(NB):
        for ref, out, first in ((x3, qx, xleft), (s3, qs, zb)):
            left = first if m == 0 else ref[1, :, 256 * m - 128 : 256 * m][:, 96:128]
            right = zb if m == NB - 1 else ref[1, :, 256 * m + 256 : 256 * m + 384][:, 0:C]
            q = jnp.concatenate([left, right, left, right], 1)
            out[:, 256 * m : 256 * m + 128] = jnp.where(lane128 < 64, down(q), q)
            out[:, 256 * m + 128 : 256 * m + 256] = up(q)
    for n in range(24):
        left = xleft if n == 0 else x3[1, :, 128 * (n - 1) : 128 * n][:, 96:128]
        xp[:, 128 * n : 128 * n + 128] = jnp.concatenate(
            [left, x3[1, :, 128 * n : 128 * n + 128][:, 0:96]], 1
        )

    bias_row = jnp.concatenate([bias[...]] * 8, 1)
    out_copies = []
    for m in range(NB):
        blk = slice(256 * m, 256 * m + 256)
        y = dot(x3[0, :, blk], bands[0]) + dot(x3[1, :, blk], bands[1])
        y = y + dot(x3[2, :, blk], bands[2]) + dot(qx[:, blk], wq) + bias_row
        y = (y * wet[:, blk].astype(F32)).astype(BF)
        lanes = LAST if m == NB - 1 else 256
        for s in range(SL):
            yo[s, :, 256 * m : 256 * m + lanes] = y[G * s : G * s + T, :lanes]
    for s in range(SL):
        out_copies.append(pltpu.make_async_copy(yo.at[s], y_hbm.at[0, s], out_sem.at[0, s]))
        out_copies[-1].start()

    row8 = lax.broadcasted_iota(jnp.int32, (8, 256), 0)
    for m in range(NB):
        blk = slice(256 * m, 256 * m + 256)
        y = dot_t(s3[0, :, blk], bands[2]) + dot_t(s3[1, :, blk], bands[1])
        y = y + dot_t(s3[2, :, blk], bands[0]) + dot_t(qs[:, blk], wqb)
        if m == 0:
            y = y + rim_first
        if m == NB - 1:
            y = y + rim_last
        parts = []
        for s in range(SL):
            top = jnp.where(row8 == 0, rim[0][8 * m + s : 8 * m + s + 1], 0.0)
            low = jnp.where(row8 == 1, rim[1][8 * m + s : 8 * m + s + 1], 0.0)
            parts.append(y[G * s : G * s + 8] + top)
            parts.append(y[G * s + 8 : G * s + 88])
            parts.append(y[G * s + 88 : G * s + 96] + low)
        y = jnp.concatenate(parts, 0)
        y = (y * wet[:, blk].astype(F32)).astype(BF)
        lanes = LAST if m == NB - 1 else 256
        for s in range(SL):
            go[s, :, 256 * m : 256 * m + lanes] = y[G * s : G * s + T, :lanes]
    for s in range(SL):
        out_copies.append(pltpu.make_async_copy(go.at[s], gi_hbm.at[0, s], out_sem.at[1, s]))
        out_copies[-1].start()

    grad = jnp.zeros((384, 256), F32)
    for m in range(23):
        sv = jnp.concatenate(
            [s3[2 - a, :, 128 * m : 128 * m + 128] for a in range(3)], 1
        )
        xv = xp[:, 128 * m : 128 * m + 256]
        grad = grad + lax.dot_general(
            sv, xv, (((0,), (0,)), ((), ())), preferred_element_type=F32
        )
    for a in range(3):
        total = None
        for j in range(4):
            piece = grad[128 * a + C * j : 128 * a + C * j + C, C * j : C * j + 96]
            total = piece if total is None else total + piece
        part_out[C * a : C * a + C] = jnp.concatenate([total, jnp.zeros((C, C), F32)], 1)
    row = jnp.sum(bias_acc, 0, keepdims=True)
    row = row[:, 0:128] + row[:, 128:256]
    row = row[:, 0:64] + row[:, 64:128]
    row = row[:, 0:C] + row[:, C : 2 * C]
    low = jnp.concatenate([row, jnp.zeros((1, 96), F32)], 1)
    part_out[96:128] = jnp.concatenate([low, jnp.zeros((31, 128), F32)], 0)
    for copy in out_copies:
        copy.wait()


def local_part(x, g, wa, consts, weight, bias, got, neighbours, reversal):
    any_ = pl.BlockSpec(memory_space=pl.ANY)
    vm = pl.BlockSpec(memory_space=pltpu.VMEM)
    sm = pl.BlockSpec(memory_space=pltpu.SMEM)
    tiles = jax.ShapeDtypeStruct((1, SL, T, W), BF)
    return pl.pallas_call(
        main_kernel,
        in_specs=[sm, sm, any_, any_] + [vm] * 10,
        out_specs=[any_, any_, vm],
        out_shape=[tiles, tiles, jax.ShapeDtypeStruct((128, 128), F32)],
        scratch_shapes=[
            pltpu.VMEM((SL, T, W), BF),
            pltpu.VMEM((SL, T, W), BF),
            pltpu.VMEM((3, R, WP), BF),
            pltpu.VMEM((3, R, WP), BF),
            pltpu.VMEM((R, WP), BF),
            pltpu.VMEM((R, WP), BF),
            pltpu.VMEM((R, WP), BF),
            pltpu.VMEM((R, WP), BF),
            pltpu.VMEM((2, 2, SL, G, 128), F32),
            pltpu.SemaphoreType.DMA((2, SL)),
            pltpu.SemaphoreType.DMA((2, SL)),
        ],
        compiler_params=pltpu.CompilerParams(vmem_limit_bytes=VMEM_LIMIT),
    )(neighbours, reversal, x, g, wa, *consts, weight, bias, *got)


def sum_kernel(n_face, n_tile, n_dp, scale, p_ref, w_out, b_out, got1, mine, got2, full, s1, r1, s2, r2, s3, r3):
    f, t, d = lax.axis_index("face"), lax.axis_index("tile"), lax.axis_index("dp")
    n_plane = n_face * n_dp
    me = f * n_dp + d

    def tile_peer(k):
        return (f, lax.rem(t + k, n_tile), d)

    def plane_peer(k):
        q = lax.rem(me + k, n_plane)
        return (q // n_dp, t, lax.rem(q, n_dp))

    barrier = pltpu.get_barrier_semaphore()
    for k in range(1, n_tile):
        pl.semaphore_signal(barrier, inc=1, device_id=tile_peer(k), device_id_type=MESH)
    for k in range(1, n_plane):
        pl.semaphore_signal(barrier, inc=1, device_id=plane_peer(k), device_id_type=MESH)
    pl.semaphore_wait(barrier, n_tile + n_plane - 2)

    def rows8(i):
        return pl.ds(pl.multiple_of(i * 8, 8), 8)

    sends = []
    for k in range(1, n_tile):
        u = lax.rem(t + k, n_tile)
        copy = pltpu.make_async_remote_copy(
            src_ref=p_ref.at[rows8(u)],
            dst_ref=got1.at[k],
            send_sem=s1.at[k],
            recv_sem=r1.at[k],
            device_id=tile_peer(k),
            device_id_type=MESH,
        )
        copy.start()
        sends.append(copy)
    got1[0] = p_ref[rows8(t)]
    for copy in sends:
        copy.wait()
    total = got1[0]
    for k in range(1, n_tile):
        total = total + got1[k]
    mine[...] = total

    sends = []
    for k in range(1, n_plane):
        copy = pltpu.make_async_remote_copy(
            src_ref=mine,
            dst_ref=got2.at[me],
            send_sem=s2.at[k],
            recv_sem=r2.at[k],
            device_id=plane_peer(k),
            device_id_type=MESH,
        )
        copy.start()
        sends.append(copy)
    got2[me] = mine[...]
    for copy in sends:
        copy.wait()
    total = got2[0]
    for k in range(1, n_plane):
        total = total + got2[k]
    full[rows8(t)] = total * scale

    sends = []
    for k in range(1, n_tile):
        copy = pltpu.make_async_remote_copy(
            src_ref=full.at[rows8(t)],
            dst_ref=full.at[rows8(t)],
            send_sem=s3.at[k],
            recv_sem=r3.at[k],
            device_id=tile_peer(k),
            device_id_type=MESH,
        )
        copy.start()
        sends.append(copy)
    for copy in sends:
        copy.wait()
    for a in range(3):
        w_out[96 * a : 96 * a + 96] = full[C * a : C * a + C].T[0:96]
    b_out[...] = full[96:97, 0:C]


def device_sum(part, n_face, n_tile, n_dp, scale):
    vm = pl.BlockSpec(memory_space=pltpu.VMEM)
    n_plane = n_face * n_dp
    dma = pltpu.SemaphoreType.DMA
    return pl.pallas_call(
        functools.partial(sum_kernel, n_face, n_tile, n_dp, scale),
        in_specs=[vm],
        out_specs=[vm, vm],
        out_shape=[
            jax.ShapeDtypeStruct((9 * C, C), F32),
            jax.ShapeDtypeStruct((1, C), F32),
        ],
        scratch_shapes=[
            pltpu.VMEM((n_tile, 8, 128), F32),
            pltpu.VMEM((8, 128), F32),
            pltpu.VMEM((n_plane, 8, 128), F32),
            pltpu.VMEM((128, 128), F32),
            dma((n_tile,)),
            dma((n_tile,)),
            dma((n_plane,)),
            dma((n_plane,)),
            dma((n_tile,)),
            dma((n_tile,)),
        ],
        compiler_params=pltpu.CompilerParams(collective_id=0, has_side_effects=True),
    )(part)


def passed_along(block, axis, distance):
    n = lax.axis_size(axis)
    return lax.ppermute(block, axis, [((i - distance) % n, i) for i in range(n)])


def per_device(
    inputs, cotangent, conv_weight, out_bias, cell_area, land_mask, neighbours, reversal, wet_count
):
    occupied = jnp.arange(SL, dtype=jnp.int32) < wet_count[0]
    wa = jnp.where((land_mask != 0) & occupied[:, None], cell_area, 0.0).reshape(SL, T, T)
    spread = jnp.asarray(spread_matrix())
    flip_l = jnp.asarray(flip_lanes_matrix())
    flip_r = jnp.asarray(flip_rows_matrix())
    r0, r1, c0, c1 = edges(inputs, cotangent, wa, spread)
    got = (
        passed_along(r1, "tile", -1),
        passed_along(r0, "tile", 1),
        passed_along(c0, "face", -1),
        passed_along(c1, "face", 1),
    )
    outputs, input_grad, part = local_part(
        inputs,
        cotangent,
        wa,
        (spread, flip_l, flip_r),
        conv_weight,
        out_bias[None],
        got,
        neighbours,
        reversal,
    )
    n_face, n_tile, n_dp = (lax.axis_size(a) for a in ("face", "tile", "dp"))
    scale = 1.0 / math.sqrt(n_dp * n_face * n_tile * SL * T * T)
    weight_grad, bias_grad = device_sum(part, n_face, n_tile, n_dp, scale)
    return outputs, input_grad, weight_grad, bias_grad[0]


def solution(mesh):
    return jax.shard_map(
        per_device,
        mesh=mesh,
        in_specs=(
            P("dp", ("face", "tile"), None, None),
            P("dp", ("face", "tile"), None, None),
            P(),
            P(),
            P(("face", "tile"), None),
            P(("face", "tile"), None),
            P(("face", "tile"), None),
            P(("face", "tile"), None),
            P(("face", "tile")),
        ),
        out_specs=(
            P("dp", ("face", "tile"), None, None),
            P("dp", ("face", "tile"), None, None),
            P(),
            P(),
        ),
        check_vma=False,
    )
```

```python
import functools
import math

import jax
import jax.numpy as jnp
import ml_dtypes
import numpy as np
from jax import lax
from jax.experimental import pallas as pl
from jax.experimental.pallas import tpu as pltpu
from jax.sharding import PartitionSpec as P

MESH = pl.DeviceIdType.MESH
BF = jnp.bfloat16
F32 = jnp.float32
T = 90
C = 32
SL = 6
G = 96
R = SL * G
W = T * C
WP = 3072
NB = 12
LAST = W - 11 * 256
VMEM_LIMIT = 60 * 2**20
XW = WP + 256


def spread_matrix():
    m = np.zeros((256, WP), np.float32)
    for j in range(T):
        m[j, j * C : (j + 1) * C] = 1
        m[128 + j, j * C : (j + 1) * C] = 1
    return m.astype(ml_dtypes.bfloat16)


def flip_lanes_matrix():
    m = np.zeros((256, 128), np.float32)
    for q in range(4):
        for k in range(C):
            m[C * (5 - q) + k, C * q + k] = 1
    return m.astype(ml_dtypes.bfloat16)


def flip_rows_matrix():
    m = np.zeros((G, G), np.float32)
    for i in range(T):
        m[i, T - 1 - i] = 1
    return m.astype(ml_dtypes.bfloat16)


def dot(a, b):
    return jnp.dot(a, b, preferred_element_type=F32)


def dot_t(a, b):
    return lax.dot_general(a, b, (((1,), (1,)), ((), ())), preferred_element_type=F32)


def split_hi_lo(v):
    hi = v.astype(BF)
    lo = (v - hi.astype(F32)).astype(BF)
    return hi, lo


def device_kernel(
    sizes,
    nb,
    rev,
    x_hbm,
    g_hbm,
    wa,
    spread,
    flip_l,
    flip_r,
    weight_t,
    bias,
    y_hbm,
    gi_hbm,
    w_out,
    b_out,
    xs,
    gs,
    x1,
    s3,
    xp,
    wet,
    cols,
    row_out,
    row_in,
    col_out,
    col_in,
    rim,
    gacc,
    part,
    got1,
    mine,
    got2,
    full,
    in_sem,
    out_sem,
    halo_s,
    halo_r,
    s_sem1,
    r_sem1,
    s_sem2,
    r_sem2,
    s_sem3,
    r_sem3,
):
    n_face, n_tile, n_dp, scale = sizes
    f, t, d = lax.axis_index("face"), lax.axis_index("tile"), lax.axis_index("dp")
    n_plane = n_face * n_dp
    me = f * n_dp + d

    def tile_peer(k):
        return (f, lax.rem(t + k, n_tile), d)

    def face_peer(k):
        return (lax.rem(f + k, n_face), t, d)

    def plane_peer(k):
        q = lax.rem(me + k, n_plane)
        return (q // n_dp, t, lax.rem(q, n_dp))

    copies = []
    for s in range(SL):
        copies.append(pltpu.make_async_copy(x_hbm.at[0, s], xs.at[s], in_sem.at[0, s]))
        copies.append(pltpu.make_async_copy(g_hbm.at[0, s], gs.at[s], in_sem.at[1, s]))
    for copy in copies:
        copy.start()

    barrier = pltpu.get_barrier_semaphore()
    for k in range(1, n_tile):
        pl.semaphore_signal(barrier, inc=1, device_id=tile_peer(k), device_id_type=MESH)
    for k in range(1, n_plane):
        pl.semaphore_signal(barrier, inc=1, device_id=plane_peer(k), device_id_type=MESH)

    area = []
    for s in range(SL):
        v = jnp.concatenate([wa[s], jnp.zeros((G - T, T), F32)], 0)
        area.append(jnp.concatenate([v, jnp.zeros((G, 128 - T), F32)], 1))
    hi, lo = split_hi_lo(jnp.concatenate(area, 0))
    area = jnp.concatenate([hi, lo], 1)

    w = weight_t[...].astype(F32)
    w = jnp.concatenate([w, jnp.zeros((C, 96), F32)], 1).T[0 : 9 * C]

    def tap(a, c):
        start = (3 * a + c) * C
        return w[start : start + C]

    def band(a, cells_in, shift, mirror=False):
        rows_iota = lax.broadcasted_iota(jnp.int32, (256, cells_in * C), 0) // C
        lanes_iota = lax.broadcasted_iota(jnp.int32, (256, cells_in * C), 1) // C - shift
        which = rows_iota - lanes_iota + 1
        if mirror:
            which = 2 - which
        out = jnp.zeros((256, cells_in * C), F32)
        for c in range(3):
            wide = jnp.concatenate([tap(a, c)] * 4, 1)
            wide = jnp.concatenate([wide] * (cells_in // 4), 1)
            out = jnp.where(which == c, jnp.concatenate([wide] * 8, 0), out)
        return out.astype(BF)

    bands = [band(a, 8, 0) for a in range(3)]
    z32 = jnp.zeros((C, C), F32)
    z64 = jnp.zeros((C, 192), F32)
    wq_rows = []
    for a in range(3):
        wq_rows.append(jnp.concatenate([tap(a, 0), z32, z64], 1))
        wq_rows.append(jnp.concatenate([z64, z32, tap(a, 2)], 1))
    wq = jnp.concatenate(wq_rows + [jnp.zeros((64, 256), F32)], 0).astype(BF)
    gl = jnp.concatenate([v for a in range(3) for v in (tap(2 - a, 2), z32)] + [z32, z32], 1)
    gr = jnp.concatenate([v for a in range(3) for v in (z32, tap(2 - a, 0))] + [z32, z32], 1)
    wqb = jnp.concatenate([gl, jnp.zeros((192, 256), F32), gr], 0).astype(BF)

    for copy in copies:
        copy.wait()

    zrow = jnp.zeros((2, 256), BF)
    for side, row in ((0, 0), (1, T - 1)):
        lhs = jnp.concatenate([area[G * s + row : G * s + row + 1] for s in range(SL)] + [zrow], 0)
        wide = dot(lhs, spread[...])
        for place, ref in ((0, xs), (8, gs)):
            v = [ref[s, row : row + 1, :].astype(F32) for s in range(SL)]
            v = jnp.concatenate(v + [jnp.zeros((2, W), F32)], 0)
            v = jnp.concatenate([v, jnp.zeros((8, WP - W), F32)], 1)
            v = v * wide if place else v
            v = jnp.where(wide > 0, v, 0.0)
            if place == 0:
                kept = v
            else:
                row_out[side] = jnp.concatenate([kept, v], 0).astype(BF)
    pad = jnp.zeros((G - T, 128), BF)
    for side, col in ((0, 0), (1, T - 1)):
        for s in range(SL):
            e = jnp.broadcast_to(wa[s, :, col : col + 1], (T, C))
            xv = jnp.where(e > 0, xs[s, :, C * col : C * col + C].astype(F32), 0.0)
            gv = jnp.where(e > 0, e * gs[s, :, C * col : C * col + C].astype(F32), 0.0)
            v = jnp.concatenate([xv, gv, jnp.zeros((T, 64), F32)], 1).astype(BF)
            col_out[side, s * G : (s + 1) * G] = jnp.concatenate([v, pad], 0)

    pl.semaphore_wait(barrier, n_tile + n_plane - 2)
    halo = []
    for src, dst, k, target in (
        (row_out.at[1], row_in.at[0], 0, tile_peer(n_tile - 1)),
        (row_out.at[0], row_in.at[1], 1, tile_peer(1)),
        (col_out.at[0], col_in.at[0], 2, face_peer(n_face - 1)),
        (col_out.at[1], col_in.at[1], 3, face_peer(1)),
    ):
        copy = pltpu.make_async_remote_copy(
            src_ref=src,
            dst_ref=dst,
            send_sem=halo_s.at[k],
            recv_sem=halo_r.at[k],
            device_id=target,
            device_id_type=MESH,
        )
        copy.start()
        halo.append(copy)

    def fetch(ref, m, lanes):
        parts = []
        for s in range(SL):
            start = 256 * m if isinstance(m, int) else pl.multiple_of(256 * m, 256)
            v = ref[s, :, pl.ds(start, lanes)].astype(F32)
            if lanes < 256:
                v = jnp.concatenate([v, jnp.zeros((T, 256 - lanes), F32)], 1)
            parts.append(v)
            parts.append(jnp.zeros((G - T, 256), F32))
        return jnp.concatenate(parts, 0)

    def down(v):
        return jnp.concatenate([v[R - 1 :], v[: R - 1]], 0)

    def up(v):
        return jnp.concatenate([v[1:], v[:1]], 0)

    def at(base, size, unit=128):
        return pl.ds(base if isinstance(base, int) else pl.multiple_of(base, unit), size)

    def blocks(body, first=True):
        if first:
            body(0, 256)
        else:
            pass
        lax.fori_loop(1 if first else 0, NB - 1, lambda m, c: (body(m, 256), c)[1], 0)
        body(NB - 1, LAST)

    zcol = jnp.zeros((R, 128), BF)
    for a in range(3):
        s3[a, :, 0:128] = zcol
        s3[a, :, XW - 128 : XW] = zcol
    x1[:, XW - 128 : XW] = zcol
    gacc[0:8] = jnp.zeros((8, 256), F32)

    def prepare(m, lanes):
        e = dot(area, spread[:, at(256 * m, 256)])
        blk = at(256 * m + 128, 256)
        wet[:, at(256 * m, 256)] = (e > 0).astype(F32).astype(BF)
        x1[:, blk] = jnp.where(e > 0, fetch(xs, m, lanes), 0.0).astype(BF)
        sv = jnp.where(e > 0, e * fetch(gs, m, lanes), 0.0).astype(BF)
        s3[0, :, blk] = down(sv)
        s3[1, :, blk] = sv
        s3[2, :, blk] = up(sv)
        gacc[0:8] = gacc[0:8] + jnp.sum(sv.astype(F32).reshape(R // 8, 8, 256), 0)

    blocks(prepare, first=False)
    row = jnp.sum(gacc[0:8], 0, keepdims=True)
    row = row[:, 0:128] + row[:, 128:256]
    row = row[:, 0:64] + row[:, 64:128]
    row = row[:, 0:C] + row[:, C : 2 * C]
    low = jnp.concatenate([row, jnp.zeros((1, 96), F32)], 1)
    part[96:128] = jnp.concatenate([low, jnp.zeros((31, 128), F32)], 0)

    for copy in halo:
        copy.wait()

    zr = jnp.concatenate([row_in[0], row_in[1]], 0)
    zpad = jnp.concatenate([jnp.zeros((32, 128), BF), zr], 1)
    stacked = jnp.concatenate([zpad[:, 128 * (22 - n) : 128 * (24 - n)] for n in range(23)], 0)
    turned = dot(stacked, flip_l[...]).astype(BF)
    flipped = jnp.concatenate(
        [turned[32 * n : 32 * n + 32] for n in range(23)] + [jnp.zeros((32, 128), BF)], 1
    )
    lane_i = lax.broadcasted_iota(jnp.int32, (128, 64), 1)
    row_i = lax.broadcasted_iota(jnp.int32, (128, 64), 0)
    sel = jnp.zeros((128, 64), F32)
    for s in range(SL):
        for side, halo_row in ((0, (16 * (s - 1) + 15) % 96), (1, 16 * s + 10)):
            n, r = nb[side, s], rev[side, s]
            src = 16 * side + 32 * r + lax.rem(jnp.maximum(n, 0), SL)
            src = jnp.where(n >= 0, src, -100)
            sel = jnp.where((row_i == halo_row) & (lane_i == src), 1.0, sel)
            rim_row = 96 + 16 * side + 8 * r + s
            sel = jnp.where((row_i == rim_row) & (lane_i == src + 8), 1.0, sel)
    routed = dot(sel.astype(BF), jnp.concatenate([zr, flipped], 0))
    for s in range(SL):
        rows = slice(G * s + 80, G * s + 96)
        old = x1[rows, 128 : 128 + WP].astype(F32)
        x1[rows, 128 : 128 + WP] = (old + routed[16 * s : 16 * s + 16]).astype(BF)
    hs = routed[96:128]
    hs = jnp.concatenate([jnp.zeros((32, 128), F32), hs, jnp.zeros((32, 128), F32)], 1)
    for side, a in ((0, 2), (1, 0)):
        total = None
        for r in range(2):
            rows = hs[16 * side + 8 * r : 16 * side + 8 * r + 8]
            lhs = jnp.concatenate(
                [rows[:, 256 * m : 256 * m + 512] for m in range(NB)], 0
            ).astype(BF)
            part_sum = dot_t(lhs, band(a, 16, 4, mirror=(r == 1)))
            total = part_sum if total is None else total + part_sum
        rim[side] = total.astype(BF).astype(F32)

    for side in range(2):
        flat = jnp.concatenate([col_in[side, s * G : (s + 1) * G] for s in range(SL)], 1)
        back = dot(flip_r[...], flat)
        for s in range(SL):
            cols[side, 0, s] = col_in[side, s * G : (s + 1) * G].astype(F32)
            cols[side, 1, s] = back[:, 128 * s : 128 * s + 128]
    ecol, xleft, xright = [], [], []
    for s in range(SL):
        got = []
        pieces = []
        for side in range(2):
            n, r = nb[2 + side, s], rev[2 + side, s]
            v = cols[side, r, lax.rem(jnp.maximum(n, 0), SL)]
            v = jnp.where(n >= 0, v, 0.0)
            got.append(v)
            pieces.append(jnp.where(r == 0, v, 0.0)[:, C : 2 * C])
            pieces.append(jnp.where(r == 1, v, 0.0)[:, C : 2 * C])
        ecol.append(jnp.concatenate(pieces, 1))
        xright.append(got[0][:, 0:C])
        xleft.append(got[1][:, 0:C])
    ecol = jnp.concatenate(ecol, 0)
    xright = jnp.concatenate(xright, 0)
    xleft = jnp.concatenate(xleft, 0)
    e3 = jnp.concatenate(
        [pltpu.roll(ecol, 1, 0), ecol, pltpu.roll(ecol, R - 1, 0)], 1
    ).astype(BF)
    v2 = jnp.concatenate(
        [v for a in range(3) for v in (tap(2 - a, 0), tap(a, 0), z32, z32)], 1
    )
    v3 = jnp.concatenate(
        [v for a in range(3) for v in (z32, z32, tap(2 - a, 2), tap(a, 2))], 1
    )
    rim_col = dot_t(e3, jnp.concatenate([v2, v3], 0).astype(BF)).astype(BF).astype(F32)
    zc = jnp.zeros((R, C), F32)
    x1[:, 0:128] = jnp.concatenate([zc, zc, zc, xleft], 1).astype(BF)
    right = at(128 + 128 * 22, 128)
    x1[:, right] = (
        x1[:, right].astype(F32) + jnp.concatenate([zc, zc, xright, zc], 1)
    ).astype(BF)

    def move(n, c):
        left = x1[:, at(128 * n, 128)][:, 96:128]
        xp[:, at(128 * n, 128)] = jnp.concatenate(
            [left, x1[:, at(128 * n + 128, 128)][:, 0:96]], 1
        )
        return c

    lax.fori_loop(0, 24, move, 0)

    gacc[...] = jnp.zeros_like(gacc)

    def outer(m, c):
        sv = jnp.concatenate([s3[2 - a, :, at(128 * m + 128, 128)] for a in range(3)], 1)
        gacc[...] += lax.dot_general(
            sv, xp[:, at(128 * m, 256)], (((0,), (0,)), ((), ())), preferred_element_type=F32
        )
        return c

    lax.fori_loop(0, 23, outer, 0)
    grad = gacc[...]
    for a in range(3):
        total = None
        for j in range(4):
            piece = grad[128 * a + C * j : 128 * a + C * j + C, C * j : C * j + 96]
            total = piece if total is None else total + piece
        part[C * a : C * a + C] = jnp.concatenate([total, jnp.zeros((C, C), F32)], 1)

    def rows8(i):
        return pl.ds(pl.multiple_of(i * 8, 8), 8)

    sends = []
    for k in range(1, n_tile):
        copy = pltpu.make_async_remote_copy(
            src_ref=part.at[rows8(lax.rem(t + k, n_tile))],
            dst_ref=got1.at[k],
            send_sem=s_sem1.at[k],
            recv_sem=r_sem1.at[k],
            device_id=tile_peer(k),
            device_id_type=MESH,
        )
        copy.start()
        sends.append(copy)

    def beside(ref, m):
        mid = ref[:, at(256 * m, 128)][:, 96:128]
        far = ref[:, at(256 * m + 384, 128)][:, 0:C]
        q = jnp.concatenate([mid, far, mid, far], 1)
        lane = lax.broadcasted_iota(jnp.int32, (R, 128), 1)
        return jnp.concatenate([jnp.where(lane < 64, down(q), q), up(q)], 1)

    bias_row = jnp.concatenate([bias[...]] * 8, 1)

    def forward(m, lanes):
        xv = x1[:, at(256 * m + 128, 256)]
        y = dot(down(xv), bands[0]) + dot(xv, bands[1])
        y = y + dot(up(xv), bands[2]) + dot(beside(x1, m), wq) + bias_row
        y = (y * wet[:, at(256 * m, 256)].astype(F32)).astype(BF)
        for s in range(SL):
            xs[s, :, at(256 * m, lanes)] = y[G * s : G * s + T, :lanes]

    blocks(forward, first=False)
    out_copies = []
    for s in range(SL):
        out_copies.append(pltpu.make_async_copy(xs.at[s], y_hbm.at[0, s], out_sem.at[0, s]))
        out_copies[-1].start()

    for copy in sends:
        copy.wait()
    total = part[rows8(t)]
    for k in range(1, n_tile):
        total = total + got1[k]
    mine[...] = total
    sends = []
    for k in range(1, n_plane):
        copy = pltpu.make_async_remote_copy(
            src_ref=mine,
            dst_ref=got2.at[me],
            send_sem=s_sem2.at[k],
            recv_sem=r_sem2.at[k],
            device_id=plane_peer(k),
            device_id_type=MESH,
        )
        copy.start()
        sends.append(copy)
    got2[me] = total

    row8 = lax.broadcasted_iota(jnp.int32, (8, 256), 0)
    z6 = jnp.zeros((R, 192), F32)

    def backward(m, lanes):
        blk = at(256 * m + 128, 256)
        y = dot_t(s3[0, :, blk], bands[2]) + dot_t(s3[1, :, blk], bands[1])
        y = y + dot_t(s3[2, :, blk], bands[0]) + dot_t(beside(s3.at[1], m), wqb)
        if isinstance(m, int) and m == 0:
            y = y + jnp.concatenate([rim_col[:, C : 2 * C], zc, z6], 1)
        if isinstance(m, int) and m == NB - 1:
            y = y + jnp.concatenate([zc, rim_col[:, 0:C], z6], 1)
        parts = []
        tops = rim[0, at(8 * m, 8, 8), :]
        lows = rim[1, at(8 * m, 8, 8), :]
        for s in range(SL):
            parts.append(y[G * s : G * s + 8] + jnp.where(row8 == 0, tops[s : s + 1], 0.0))
            parts.append(y[G * s + 8 : G * s + 88])
            parts.append(y[G * s + 88 : G * s + 96] + jnp.where(row8 == 1, lows[s : s + 1], 0.0))
        y = jnp.concatenate(parts, 0)
        y = (y * wet[:, at(256 * m, 256)].astype(F32)).astype(BF)
        for s in range(SL):
            gs[s, :, at(256 * m, lanes)] = y[G * s : G * s + T, :lanes]

    backward(0, 256)
    lax.fori_loop(1, 6, lambda m, c: (backward(m, 256), c)[1], 0)

    for copy in sends:
        copy.wait()
    total = got2[0]
    for k in range(1, n_plane):
        total = total + got2[k]
    full[rows8(t)] = total * scale
    sends = []
    for k in range(1, n_tile):
        copy = pltpu.make_async_remote_copy(
            src_ref=full.at[rows8(t)],
            dst_ref=full.at[rows8(t)],
            send_sem=s_sem3.at[k],
            recv_sem=r_sem3.at[k],
            device_id=tile_peer(k),
            device_id_type=MESH,
        )
        copy.start()
        sends.append(copy)

    lax.fori_loop(6, NB - 1, lambda m, c: (backward(m, 256), c)[1], 0)
    backward(NB - 1, LAST)
    for s in range(SL):
        out_copies.append(pltpu.make_async_copy(gs.at[s], gi_hbm.at[0, s], out_sem.at[1, s]))
        out_copies[-1].start()

    for copy in sends:
        copy.wait()
    for a in range(3):
        w_out[a] = full[C * a : C * a + C]
    b_out[...] = full[96:97, 0:C]
    for copy in out_copies:
        copy.wait()


def per_device(
    inputs, cotangent, conv_weight, out_bias, cell_area, land_mask, neighbours, reversal, wet_count
):
    occupied = jnp.arange(SL, dtype=jnp.int32) < wet_count[0]
    wa = jnp.where((land_mask != 0) & occupied[:, None], cell_area, 0.0).reshape(SL, T, T)
    n_face, n_tile, n_dp = (lax.axis_size(a) for a in ("face", "tile", "dp"))
    n_plane = n_face * n_dp
    scale = 1.0 / math.sqrt(n_dp * n_face * n_tile * SL * T * T)
    any_ = pl.BlockSpec(memory_space=pl.ANY)
    vm = pl.BlockSpec(memory_space=pltpu.VMEM)
    sm = pl.BlockSpec(memory_space=pltpu.SMEM)
    tiles = jax.ShapeDtypeStruct((1, SL, T, W), BF)
    dma = pltpu.SemaphoreType.DMA
    outputs, input_grad, w_sum, b_sum = pl.pallas_call(
        functools.partial(device_kernel, (n_face, n_tile, n_dp, scale)),
        in_specs=[sm, sm, any_, any_] + [vm] * 6,
        out_specs=[any_, any_, vm, vm],
        out_shape=[
            tiles,
            tiles,
            jax.ShapeDtypeStruct((3, C, 128), F32),
            jax.ShapeDtypeStruct((1, C), F32),
        ],
        scratch_shapes=[
            pltpu.VMEM((SL, T, W), BF),
            pltpu.VMEM((SL, T, W), BF),
            pltpu.VMEM((R, XW), BF),
            pltpu.VMEM((3, R, XW), BF),
            pltpu.VMEM((R, WP), BF),
            pltpu.VMEM((R, WP), BF),
            pltpu.VMEM((2, 2, SL, G, 128), F32),
            pltpu.VMEM((2, 16, WP), BF),
            pltpu.VMEM((2, 16, WP), BF),
            pltpu.VMEM((2, R, 128), BF),
            pltpu.VMEM((2, R, 128), BF),
            pltpu.VMEM((2, 8 * NB, 256), F32),
            pltpu.VMEM((384, 256), F32),
            pltpu.VMEM((128, 128), F32),
            pltpu.VMEM((n_tile, 8, 128), F32),
            pltpu.VMEM((8, 128), F32),
            pltpu.VMEM((n_plane, 8, 128), F32),
            pltpu.VMEM((128, 128), F32),
            dma((2, SL)),
            dma((2, SL)),
            dma((4,)),
            dma((4,)),
            dma((n_tile,)),
            dma((n_tile,)),
            dma((n_plane,)),
            dma((n_plane,)),
            dma((n_tile,)),
            dma((n_tile,)),
        ],
        compiler_params=pltpu.CompilerParams(
            vmem_limit_bytes=VMEM_LIMIT, collective_id=0, has_side_effects=True
        ),
    )(
        neighbours.T,
        reversal.T,
        inputs,
        cotangent,
        wa,
        jnp.asarray(spread_matrix()),
        jnp.asarray(flip_lanes_matrix()),
        jnp.asarray(flip_rows_matrix()),
        conv_weight.T,
        out_bias[None],
    )
    weight_grad = w_sum[:, :, 0 : 3 * C].transpose(0, 2, 1).reshape(9 * C, C)
    return outputs, input_grad, weight_grad, b_sum[0]


def solution(mesh):
    return jax.shard_map(
        per_device,
        mesh=mesh,
        in_specs=(
            P("dp", ("face", "tile"), None, None),
            P("dp", ("face", "tile"), None, None),
            P(),
            P(),
            P(("face", "tile"), None),
            P(("face", "tile"), None),
            P(("face", "tile"), None),
            P(("face", "tile"), None),
            P(("face", "tile")),
        ),
        out_specs=(
            P("dp", ("face", "tile"), None, None),
            P("dp", ("face", "tile"), None, None),
            P(),
            P(),
        ),
        check_vma=False,
    )
```

```python
import functools
import math

import jax
import jax.numpy as jnp
from jax import lax
from jax.experimental import pallas as pl
from jax.experimental.pallas import tpu as pltpu
from jax.sharding import PartitionSpec as P

MESH = pl.DeviceIdType.MESH
BF = jnp.bfloat16
F32 = jnp.float32
T = 90
C = 32
SL = 6
G = 96
R = SL * G
W = T * C
WP = 3072
NB = 12
LAST = W - 11 * 256
VMEM_LIMIT = 60 * 2**20
XW = WP + 256


def dot(a, b):
    return jnp.dot(a, b, preferred_element_type=F32)


def dot_t(a, b):
    return lax.dot_general(a, b, (((1,), (1,)), ((), ())), preferred_element_type=F32)


def split_hi_lo(v):
    hi = v.astype(BF)
    lo = (v - hi.astype(F32)).astype(BF)
    return hi, lo


def device_kernel(
    sizes,
    nb,
    rev,
    x_hbm,
    g_hbm,
    count,
    area_in,
    mask_in,
    weight_t,
    bias,
    y_hbm,
    gi_hbm,
    w_out,
    b_out,
    xs,
    gs,
    spread,
    by_row,
    area_ref,
    bands,
    wq,
    wqb,
    rim_col,
    hs_ref,
    x3,
    s3,
    xp,
    wet,
    cols,
    row_out,
    row_in,
    col_out,
    col_in,
    rim,
    gacc,
    part,
    got1,
    mine,
    got2,
    full,
    in_sem,
    out_sem,
    halo_s,
    halo_r,
    s_sem1,
    r_sem1,
    s_sem2,
    r_sem2,
    s_sem3,
    r_sem3,
):
    n_face, n_tile, n_dp, scale = sizes
    f, t, d = lax.axis_index("face"), lax.axis_index("tile"), lax.axis_index("dp")
    n_plane = n_face * n_dp
    me = f * n_dp + d

    def tile_peer(k):
        return (f, lax.rem(t + k, n_tile), d)

    def face_peer(k):
        return (lax.rem(f + k, n_face), t, d)

    def plane_peer(k):
        q = lax.rem(me + k, n_plane)
        return (q // n_dp, t, lax.rem(q, n_dp))

    copies = []
    for s in range(SL):
        copies.append(pltpu.make_async_copy(x_hbm.at[0, s], xs.at[s], in_sem.at[0, s]))
        copies.append(pltpu.make_async_copy(g_hbm.at[0, s], gs.at[s], in_sem.at[1, s]))
    for copy in copies:
        copy.start()

    barrier = pltpu.get_barrier_semaphore()
    for k in range(1, n_tile):
        pl.semaphore_signal(barrier, inc=1, device_id=tile_peer(k), device_id_type=MESH)
    for k in range(1, n_plane):
        pl.semaphore_signal(barrier, inc=1, device_id=plane_peer(k), device_id_type=MESH)

    w = weight_t[...].astype(F32)
    w = jnp.concatenate([w, jnp.zeros((C, 96), F32)], 1).T[0 : 9 * C]

    def tap(a, c):
        start = (3 * a + c) * C
        return w[start : start + C]

    def band(a, cells_in, shift, mirror=False):
        rows_iota = lax.broadcasted_iota(jnp.int32, (256, cells_in * C), 0) // C
        lanes_iota = lax.broadcasted_iota(jnp.int32, (256, cells_in * C), 1) // C - shift
        which = rows_iota - lanes_iota + 1
        if mirror:
            which = 2 - which
        out = jnp.zeros((256, cells_in * C), F32)
        for c in range(3):
            wide = jnp.concatenate([tap(a, c)] * 4, 1)
            wide = jnp.concatenate([wide] * (cells_in // 4), 1)
            out = jnp.where(which == c, jnp.concatenate([wide] * 8, 0), out)
        return out.astype(BF)

    @pl.when(t >= 0)
    def _():
        slot_i = lax.broadcasted_iota(jnp.int32, (SL, T * T), 0)
        flat = jnp.where((mask_in[...] != 0) & (slot_i < count[0]), area_in[...], 0.0)
        flat = jnp.concatenate([flat, jnp.zeros((2, T * T), F32)], 0)
        for i in range(T):
            by_row[i] = jnp.concatenate([flat[:, T * i : T * i + T], jnp.zeros((8, 128 - T), F32)], 1)
        by_row[T:G] = jnp.zeros((G - T, 8, 128), F32)
        wa = [by_row[:, s, :] for s in range(SL)]
        hi, lo = split_hi_lo(jnp.concatenate(wa, 0))
        area_ref[...] = jnp.concatenate([hi, lo], 1)

        for m in range(NB):
            r_i = lax.broadcasted_iota(jnp.int32, (256, 256), 0)
            l_i = lax.broadcasted_iota(jnp.int32, (256, 256), 1)
            hit = (r_i & 127) == (l_i >> 5) + 8 * m
            spread[:, 256 * m : 256 * m + 256] = jnp.where(hit & ((r_i & 127) < T), 1.0, 0.0).astype(BF)

        for a in range(3):
            bands[a] = band(a, 8, 0)
        z32 = jnp.zeros((C, C), F32)
        z64 = jnp.zeros((C, 192), F32)
        wq_rows = []
        for a in range(3):
            wq_rows.append(jnp.concatenate([tap(a, 0), z32, z64], 1))
            wq_rows.append(jnp.concatenate([z64, z32, tap(a, 2)], 1))
        wq[...] = jnp.concatenate(wq_rows + [jnp.zeros((64, 256), F32)], 0).astype(BF)
        gl = jnp.concatenate([v for a in range(3) for v in (tap(2 - a, 2), z32)] + [z32, z32], 1)
        gr = jnp.concatenate([v for a in range(3) for v in (z32, tap(2 - a, 0))] + [z32, z32], 1)
        wqb[...] = jnp.concatenate([gl, jnp.zeros((192, 256), F32), gr], 0).astype(BF)

    for copy in copies:
        copy.wait()

    @pl.when(t >= 0)
    def _():
        wa = [by_row[:, s, :] for s in range(SL)]
        for side, row in ((0, 0), (1, T - 1)):
            lhs = [by_row[row, s : s + 1, :] for s in range(SL)] + [jnp.zeros((2, 128), F32)]
            lhs = jnp.concatenate(split_hi_lo(jnp.concatenate(lhs, 0)), 1)
            wide = dot(lhs, spread[...])
            for place, ref in ((0, xs), (8, gs)):
                v = [ref[s, row : row + 1, :].astype(F32) for s in range(SL)]
                v = jnp.concatenate(v + [jnp.zeros((2, W), F32)], 0)
                v = jnp.concatenate([v, jnp.zeros((8, WP - W), F32)], 1)
                v = v * wide if place else v
                v = jnp.where(wide > 0, v, 0.0)
                if place == 0:
                    kept = v
                else:
                    row_out[side] = jnp.concatenate([kept, v], 0).astype(BF)
        pad = jnp.zeros((G - T, 128), BF)
        for side, col in ((0, 0), (1, T - 1)):
            for s in range(SL):
                e = jnp.broadcast_to(wa[s][0:T, col : col + 1], (T, C))
                xv = jnp.where(e > 0, xs[s, :, C * col : C * col + C].astype(F32), 0.0)
                gv = jnp.where(e > 0, e * gs[s, :, C * col : C * col + C].astype(F32), 0.0)
                v = jnp.concatenate([xv, gv, jnp.zeros((T, 64), F32)], 1).astype(BF)
                col_out[side, s * G : (s + 1) * G] = jnp.concatenate([v, pad], 0)

    pl.semaphore_wait(barrier, n_tile + n_plane - 2)
    halo = []
    for src, dst, k, target in (
        (row_out.at[1], row_in.at[0], 0, tile_peer(n_tile - 1)),
        (row_out.at[0], row_in.at[1], 1, tile_peer(1)),
        (col_out.at[0], col_in.at[0], 2, face_peer(n_face - 1)),
        (col_out.at[1], col_in.at[1], 3, face_peer(1)),
    ):
        copy = pltpu.make_async_remote_copy(
            src_ref=src,
            dst_ref=dst,
            send_sem=halo_s.at[k],
            recv_sem=halo_r.at[k],
            device_id=target,
            device_id_type=MESH,
        )
        copy.start()
        halo.append(copy)

    def fetch(ref, m, lanes):
        parts = []
        for s in range(SL):
            start = 256 * m if isinstance(m, int) else pl.multiple_of(256 * m, 256)
            v = ref[s, :, pl.ds(start, lanes)].astype(F32)
            if lanes < 256:
                v = jnp.concatenate([v, jnp.zeros((T, 256 - lanes), F32)], 1)
            parts.append(v)
            parts.append(jnp.zeros((G - T, 256), F32))
        return jnp.concatenate(parts, 0)

    def down(v):
        return jnp.concatenate([v[R - 1 :], v[: R - 1]], 0)

    def up(v):
        return jnp.concatenate([v[1:], v[:1]], 0)

    def at(base, size, unit=128):
        return pl.ds(base if isinstance(base, int) else pl.multiple_of(base, unit), size)

    def blocks(body):
        for m in range(NB):
            body(m, 256 if m < NB - 1 else LAST)

    x1 = x3.at[1]
    @pl.when(t >= 0)
    def _():
        zcol = jnp.zeros((R, 128), BF)
        for a in range(3):
            s3[a, :, 0:128] = zcol
            s3[a, :, XW - 128 : XW] = zcol
        x1[:, XW - 128 : XW] = zcol
        gacc[0:8] = jnp.zeros((8, 256), F32)

        def prepare(m, lanes):
            e = dot(area_ref[...], spread[:, at(256 * m, 256)])
            blk = at(256 * m + 128, 256)
            wet[:, at(256 * m, 256)] = (e > 0).astype(F32).astype(BF)
            x1[:, blk] = jnp.where(e > 0, fetch(xs, m, lanes), 0.0).astype(BF)
            sv = jnp.where(e > 0, e * fetch(gs, m, lanes), 0.0).astype(BF)
            s3[0, :, blk] = down(sv)
            s3[1, :, blk] = sv
            s3[2, :, blk] = up(sv)
            gacc[0:8] = gacc[0:8] + jnp.sum(sv.astype(F32).reshape(R // 8, 8, 256), 0)

        blocks(prepare)
        row = jnp.sum(gacc[0:8], 0, keepdims=True)
        row = row[:, 0:128] + row[:, 128:256]
        row = row[:, 0:64] + row[:, 64:128]
        row = row[:, 0:C] + row[:, C : 2 * C]
        low = jnp.concatenate([row, jnp.zeros((1, 96), F32)], 1)
        part[96:128] = jnp.concatenate([low, jnp.zeros((31, 128), F32)], 0)

    for copy in halo:
        copy.wait()

    r_i = lax.broadcasted_iota(jnp.int32, (256, 128), 0)
    l_i = lax.broadcasted_iota(jnp.int32, (256, 128), 1)
    flip_l = jnp.where(r_i == 160 - 32 * (l_i >> 5) + (l_i & 31), 1.0, 0.0).astype(BF)
    r_i = lax.broadcasted_iota(jnp.int32, (G, G), 0)
    l_i = lax.broadcasted_iota(jnp.int32, (G, G), 1)
    flip_r = jnp.where(r_i + l_i == T - 1, 1.0, 0.0).astype(BF)
    zr = jnp.concatenate([row_in[0], row_in[1]], 0)
    zpad = jnp.concatenate([jnp.zeros((32, 128), BF), zr], 1)
    stacked = jnp.concatenate([zpad[:, 128 * (22 - n) : 128 * (24 - n)] for n in range(23)], 0)
    turned = dot(stacked, flip_l).astype(BF)
    flipped = jnp.concatenate(
        [turned[32 * n : 32 * n + 32] for n in range(23)] + [jnp.zeros((32, 128), BF)], 1
    )
    lane_i = lax.broadcasted_iota(jnp.int32, (128, 64), 1)
    row_i = lax.broadcasted_iota(jnp.int32, (128, 64), 0)
    sel = jnp.zeros((128, 64), F32)
    for s in range(SL):
        for side, halo_row in ((0, (16 * (s - 1) + 15) % 96), (1, 16 * s + 10)):
            n, r = nb[side, s], rev[side, s]
            src = 16 * side + 32 * r + lax.rem(jnp.maximum(n, 0), SL)
            src = jnp.where(n >= 0, src, -100)
            sel = jnp.where((row_i == halo_row) & (lane_i == src), 1.0, sel)
            rim_row = 96 + 16 * side + 8 * r + s
            sel = jnp.where((row_i == rim_row) & (lane_i == src + 8), 1.0, sel)
    routed = dot(sel.astype(BF), jnp.concatenate([zr, flipped], 0))
    for s in range(SL):
        rows = slice(G * s + 80, G * s + 96)
        old = x1[rows, 128 : 128 + WP].astype(F32)
        x1[rows, 128 : 128 + WP] = (old + routed[16 * s : 16 * s + 16]).astype(BF)
    hs = routed[96:128]
    hs_ref[...] = jnp.concatenate([jnp.zeros((32, 128), F32), hs, jnp.zeros((32, 128), F32)], 1)

    for side in range(2):
        flat = jnp.concatenate([col_in[side, s * G : (s + 1) * G] for s in range(SL)], 1)
        back = dot(flip_r, flat)
        for s in range(SL):
            cols[side, 0, s] = col_in[side, s * G : (s + 1) * G].astype(F32)
            cols[side, 1, s] = back[:, 128 * s : 128 * s + 128]
    ecol, xleft, xright = [], [], []
    for s in range(SL):
        got = []
        pieces = []
        for side in range(2):
            n, r = nb[2 + side, s], rev[2 + side, s]
            v = cols[side, r, lax.rem(jnp.maximum(n, 0), SL)]
            v = jnp.where(n >= 0, v, 0.0)
            got.append(v)
            pieces.append(jnp.where(r == 0, v, 0.0)[:, C : 2 * C])
            pieces.append(jnp.where(r == 1, v, 0.0)[:, C : 2 * C])
        ecol.append(jnp.concatenate(pieces, 1))
        xright.append(got[0][:, 0:C])
        xleft.append(got[1][:, 0:C])
    rim_col[...] = jnp.concatenate(ecol, 0)
    xright = jnp.concatenate(xright, 0)
    xleft = jnp.concatenate(xleft, 0)
    zc = jnp.zeros((R, C), F32)
    x1[:, 0:128] = jnp.concatenate([zc, zc, zc, xleft], 1).astype(BF)
    right = at(128 + 128 * 22, 128)
    x1[:, right] = (
        x1[:, right].astype(F32) + jnp.concatenate([zc, zc, xright, zc], 1)
    ).astype(BF)

    def move(n):
        left = x1[:, at(128 * n, 128)][:, 96:128]
        xp[:, at(128 * n, 128)] = jnp.concatenate(
            [left, x1[:, at(128 * n + 128, 128)][:, 0:96]], 1
        )

    for n in range(24):
        move(n)

    gacc[...] = jnp.zeros_like(gacc)

    def outer(m):
        sv = jnp.concatenate([s3[2 - a, :, at(128 * m + 128, 128)] for a in range(3)], 1)
        gacc[...] += lax.dot_general(
            sv, xp[:, at(128 * m, 256)], (((0,), (0,)), ((), ())), preferred_element_type=F32
        )

    for m in range(23):
        outer(m)
    grad = gacc[...]
    for a in range(3):
        total = None
        for j in range(4):
            piece = grad[128 * a + C * j : 128 * a + C * j + C, C * j : C * j + 96]
            total = piece if total is None else total + piece
        part[C * a : C * a + C] = jnp.concatenate([total, jnp.zeros((C, C), F32)], 1)

    def rows8(i):
        return pl.ds(pl.multiple_of(i * 8, 8), 8)

    sends = []
    for k in range(1, n_tile):
        copy = pltpu.make_async_remote_copy(
            src_ref=part.at[rows8(lax.rem(t + k, n_tile))],
            dst_ref=got1.at[k],
            send_sem=s_sem1.at[k],
            recv_sem=r_sem1.at[k],
            device_id=tile_peer(k),
            device_id_type=MESH,
        )
        copy.start()
        sends.append(copy)

    def beside(ref, m):
        mid = ref[:, at(256 * m, 128)][:, 96:128]
        far = ref[:, at(256 * m + 384, 128)][:, 0:C]
        q = jnp.concatenate([mid, far, mid, far], 1)
        lane = lax.broadcasted_iota(jnp.int32, (R, 128), 1)
        return jnp.concatenate([jnp.where(lane < 64, down(q), q), up(q)], 1)

    bias_row = jnp.concatenate([bias[...]] * 8, 1)

    def forward(m, lanes):
        blk = at(256 * m + 128, 256)
        y = dot(x3[0, :, blk], bands[0]) + dot(x3[1, :, blk], bands[1])
        y = y + dot(x3[2, :, blk], bands[2]) + dot(beside(x1, m), wq[...]) + bias_row
        y = (y * wet[:, at(256 * m, 256)].astype(F32)).astype(BF)
        for s in range(SL):
            xs[s, :, at(256 * m, lanes)] = y[G * s : G * s + T, :lanes]

    @pl.when(t >= 0)
    def _():
        for side, a in ((0, 2), (1, 0)):
            total = None
            for r in range(2):
                rows = hs_ref[16 * side + 8 * r : 16 * side + 8 * r + 8]
                lhs = jnp.concatenate(
                    [rows[:, 256 * m : 256 * m + 512] for m in range(NB)], 0
                ).astype(BF)
                part_sum = dot_t(lhs, band(a, 16, 4, mirror=(r == 1)))
                total = part_sum if total is None else total + part_sum
            rim[side] = total.astype(BF).astype(F32)
        ecol = rim_col[...]
        z32 = jnp.zeros((C, C), F32)
        e3 = jnp.concatenate(
            [pltpu.roll(ecol, 1, 0), ecol, pltpu.roll(ecol, R - 1, 0)], 1
        ).astype(BF)
        v2 = jnp.concatenate(
            [v for a in range(3) for v in (tap(2 - a, 0), tap(a, 0), z32, z32)], 1
        )
        v3 = jnp.concatenate(
            [v for a in range(3) for v in (z32, z32, tap(2 - a, 2), tap(a, 2))], 1
        )
        rc = dot_t(e3, jnp.concatenate([v2, v3], 0).astype(BF)).astype(BF).astype(F32)
        rim_col[...] = jnp.concatenate([rc, jnp.zeros((R, 64), F32)], 1)
        for n in range(24):
            xv = x1[:, at(128 * n + 128, 128)]
            x3[0, :, at(128 * n + 128, 128)] = down(xv)
            x3[2, :, at(128 * n + 128, 128)] = up(xv)
        for m in range(5):
            forward(m, 256)

    for copy in sends:
        copy.wait()
    total = part[rows8(t)]
    for k in range(1, n_tile):
        total = total + got1[k]
    mine[...] = total
    sends = []
    for k in range(1, n_plane):
        copy = pltpu.make_async_remote_copy(
            src_ref=mine,
            dst_ref=got2.at[me],
            send_sem=s_sem2.at[k],
            recv_sem=r_sem2.at[k],
            device_id=plane_peer(k),
            device_id_type=MESH,
        )
        copy.start()
        sends.append(copy)
    got2[me] = total

    @pl.when(t >= 0)
    def _():
        for m in range(5, NB):
            forward(m, 256 if m < NB - 1 else LAST)

    out_copies = []
    for s in range(SL):
        out_copies.append(pltpu.make_async_copy(xs.at[s], y_hbm.at[0, s], out_sem.at[0, s]))
        out_copies[-1].start()

    row8 = lax.broadcasted_iota(jnp.int32, (8, 256), 0)
    z6 = jnp.zeros((R, 192), F32)
    zc = jnp.zeros((R, C), F32)

    def backward(m, lanes):
        blk = at(256 * m + 128, 256)
        y = dot_t(s3[0, :, blk], bands[2]) + dot_t(s3[1, :, blk], bands[1])
        y = y + dot_t(s3[2, :, blk], bands[0]) + dot_t(beside(s3.at[1], m), wqb[...])
        if isinstance(m, int) and m == 0:
            y = y + jnp.concatenate([rim_col[:, C : 2 * C], zc, z6], 1)
        if isinstance(m, int) and m == NB - 1:
            y = y + jnp.concatenate([zc, rim_col[:, 0:C], z6], 1)
        parts = []
        tops = rim[0, at(8 * m, 8, 8), :]
        lows = rim[1, at(8 * m, 8, 8), :]
        for s in range(SL):
            parts.append(y[G * s : G * s + 8] + jnp.where(row8 == 0, tops[s : s + 1], 0.0))
            parts.append(y[G * s + 8 : G * s + 88])
            parts.append(y[G * s + 88 : G * s + 96] + jnp.where(row8 == 1, lows[s : s + 1], 0.0))
        y = jnp.concatenate(parts, 0)
        y = (y * wet[:, at(256 * m, 256)].astype(F32)).astype(BF)
        for s in range(SL):
            gs[s, :, at(256 * m, lanes)] = y[G * s : G * s + T, :lanes]

    for copy in sends:
        copy.wait()
    total = got2[0]
    for k in range(1, n_plane):
        total = total + got2[k]
    full[rows8(t)] = total * scale
    sends = []
    for k in range(1, n_tile):
        copy = pltpu.make_async_remote_copy(
            src_ref=full.at[rows8(t)],
            dst_ref=full.at[rows8(t)],
            send_sem=s_sem3.at[k],
            recv_sem=r_sem3.at[k],
            device_id=tile_peer(k),
            device_id_type=MESH,
        )
        copy.start()
        sends.append(copy)

    @pl.when(t >= 0)
    def _():
        for m in range(NB):
            backward(m, 256 if m < NB - 1 else LAST)

    for s in range(SL):
        out_copies.append(pltpu.make_async_copy(gs.at[s], gi_hbm.at[0, s], out_sem.at[1, s]))
        out_copies[-1].start()

    for copy in sends:
        copy.wait()
    w_out[...] = jnp.concatenate([full[C * a : C * a + C, 0 : 3 * C] for a in range(3)], 1)
    b_out[...] = full[96:97, 0:C]
    for copy in out_copies:
        copy.wait()


def settle_kernel(y_in, gi_in, w_in, b_in, y, gi, w, b, ys, gis, in_sem, out_sem):
    pairs = ((y_in, ys, y), (gi_in, gis, gi))
    loads = [
        pltpu.make_async_copy(src.at[0, s], mid.at[s], in_sem.at[i, s])
        for s in range(SL)
        for i, (src, mid, dst) in enumerate(pairs)
    ]
    stores = [
        pltpu.make_async_copy(mid.at[s], dst.at[0, s], out_sem.at[i, s])
        for s in range(SL)
        for i, (src, mid, dst) in enumerate(pairs)
    ]
    for load in loads:
        load.start()
    w[...] = w_in[...]
    b[...] = b_in[...]
    for load, store in zip(loads, stores):
        load.wait()
        store.start()
    for store in stores:
        store.wait()


def settle(y, gi, w, b):
    any_ = pl.BlockSpec(memory_space=pl.ANY)
    vm = pl.BlockSpec(memory_space=pltpu.VMEM)
    return pl.pallas_call(
        settle_kernel,
        in_specs=[any_, any_, vm, vm],
        out_specs=[any_, any_, vm, vm],
        out_shape=[jax.ShapeDtypeStruct(v.shape, v.dtype) for v in (y, gi, w, b)],
        scratch_shapes=[
            pltpu.VMEM((SL, T, W), BF),
            pltpu.VMEM((SL, T, W), BF),
            pltpu.SemaphoreType.DMA((2, SL)),
            pltpu.SemaphoreType.DMA((2, SL)),
        ],
        compiler_params=pltpu.CompilerParams(vmem_limit_bytes=VMEM_LIMIT),
    )(y, gi, w, b)


def per_device(
    inputs, cotangent, conv_weight, out_bias, cell_area, land_mask, neighbours, reversal, wet_count
):
    n_face, n_tile, n_dp = (lax.axis_size(a) for a in ("face", "tile", "dp"))
    n_plane = n_face * n_dp
    scale = 1.0 / math.sqrt(n_dp * n_face * n_tile * SL * T * T)
    any_ = pl.BlockSpec(memory_space=pl.ANY)
    vm = pl.BlockSpec(memory_space=pltpu.VMEM)
    sm = pl.BlockSpec(memory_space=pltpu.SMEM)
    tiles = jax.ShapeDtypeStruct((1, SL, T, W), BF)
    dma = pltpu.SemaphoreType.DMA
    outputs, input_grad, w_sum, b_sum = pl.pallas_call(
        functools.partial(device_kernel, (n_face, n_tile, n_dp, scale)),
        in_specs=[sm, sm, any_, any_, sm] + [vm] * 4,
        out_specs=[any_, any_, vm, vm],
        out_shape=[
            tiles,
            tiles,
            jax.ShapeDtypeStruct((C, 9 * C), F32),
            jax.ShapeDtypeStruct((1, C), F32),
        ],
        scratch_shapes=[
            pltpu.VMEM((SL, T, W), BF),
            pltpu.VMEM((SL, T, W), BF),
            pltpu.VMEM((256, WP), BF),
            pltpu.VMEM((G, 8, 128), F32),
            pltpu.VMEM((R, 256), BF),
            pltpu.VMEM((3, 256, 256), BF),
            pltpu.VMEM((256, 256), BF),
            pltpu.VMEM((256, 256), BF),
            pltpu.VMEM((R, 128), F32),
            pltpu.VMEM((32, XW), F32),
            pltpu.VMEM((3, R, XW), BF),
            pltpu.VMEM((3, R, XW), BF),
            pltpu.VMEM((R, WP), BF),
            pltpu.VMEM((R, WP), BF),
            pltpu.VMEM((2, 2, SL, G, 128), F32),
            pltpu.VMEM((2, 16, WP), BF),
            pltpu.VMEM((2, 16, WP), BF),
            pltpu.VMEM((2, R, 128), BF),
            pltpu.VMEM((2, R, 128), BF),
            pltpu.VMEM((2, 8 * NB, 256), F32),
            pltpu.VMEM((384, 256), F32),
            pltpu.VMEM((128, 128), F32),
            pltpu.VMEM((n_tile, 8, 128), F32),
            pltpu.VMEM((8, 128), F32),
            pltpu.VMEM((n_plane, 8, 128), F32),
            pltpu.VMEM((128, 128), F32),
            dma((2, SL)),
            dma((2, SL)),
            dma((4,)),
            dma((4,)),
            dma((n_tile,)),
            dma((n_tile,)),
            dma((n_plane,)),
            dma((n_plane,)),
            dma((n_tile,)),
            dma((n_tile,)),
        ],
        compiler_params=pltpu.CompilerParams(
            vmem_limit_bytes=VMEM_LIMIT, collective_id=0, has_side_effects=True
        ),
    )(
        neighbours.T,
        reversal.T,
        inputs,
        cotangent,
        wet_count,
        cell_area,
        land_mask,
        conv_weight.T,
        out_bias[None],
    )
    outputs, input_grad, w_sum, b_sum = settle(outputs, input_grad, w_sum, b_sum)
    return outputs, input_grad, w_sum.T, b_sum[0]


def solution(mesh):
    return jax.shard_map(
        per_device,
        mesh=mesh,
        in_specs=(
            P("dp", ("face", "tile"), None, None),
            P("dp", ("face", "tile"), None, None),
            P(),
            P(),
            P(("face", "tile"), None),
            P(("face", "tile"), None),
            P(("face", "tile"), None),
            P(("face", "tile"), None),
            P(("face", "tile")),
        ),
        out_specs=(
            P("dp", ("face", "tile"), None, None),
            P("dp", ("face", "tile"), None, None),
            P(),
            P(),
        ),
        check_vma=False,
    )
```

```python
import functools
import math

import jax
import jax.numpy as jnp
from jax import lax
from jax.experimental import pallas as pl
from jax.experimental.pallas import tpu as pltpu
from jax.sharding import PartitionSpec as P

MESH = pl.DeviceIdType.MESH
BF = jnp.bfloat16
F32 = jnp.float32
T = 90
C = 32
SL = 6
G = 96
R = SL * G
W = T * C
WP = 3072
NB = 12
LAST = W - 11 * 256
VMEM_LIMIT = 60 * 2**20
XW = WP + 256


def dot(a, b):
    return jnp.dot(a, b, preferred_element_type=F32)


def dot_t(a, b):
    return lax.dot_general(a, b, (((1,), (1,)), ((), ())), preferred_element_type=F32)


def split_hi_lo(v):
    hi = v.astype(BF)
    lo = (v - hi.astype(F32)).astype(BF)
    return hi, lo


def device_kernel(
    sizes,
    nb,
    rev,
    x_hbm,
    g_hbm,
    count,
    area_in,
    mask_in,
    weight_t,
    bias,
    y_hbm,
    gi_hbm,
    w_out,
    b_out,
    xs,
    gs,
    spread,
    by_row,
    area_ref,
    bands,
    wq,
    wqb,
    rim_col,
    hs_ref,
    x3,
    s3,
    xp,
    wet,
    cols,
    row_out,
    row_in,
    col_out,
    col_in,
    rim,
    gacc,
    part,
    got1,
    mine,
    got2,
    full,
    in_sem,
    out_sem,
    halo_s,
    halo_r,
    s_sem1,
    r_sem1,
    s_sem2,
    r_sem2,
    s_sem3,
    r_sem3,
):
    n_face, n_tile, n_dp, scale = sizes
    f, t, d = lax.axis_index("face"), lax.axis_index("tile"), lax.axis_index("dp")
    n_plane = n_face * n_dp
    me = f * n_dp + d

    def tile_peer(k):
        return (f, lax.rem(t + k, n_tile), d)

    def face_peer(k):
        return (lax.rem(f + k, n_face), t, d)

    def plane_peer(k):
        q = lax.rem(me + k, n_plane)
        return (q // n_dp, t, lax.rem(q, n_dp))

    copies = []
    for s in range(SL):
        copies.append(pltpu.make_async_copy(x_hbm.at[0, s], xs.at[s], in_sem.at[0, s]))
        copies.append(pltpu.make_async_copy(g_hbm.at[0, s], gs.at[s], in_sem.at[1, s]))
    for copy in copies:
        copy.start()

    barrier = pltpu.get_barrier_semaphore()
    for k in range(1, n_tile):
        pl.semaphore_signal(barrier, inc=1, device_id=tile_peer(k), device_id_type=MESH)
    for k in range(1, n_plane):
        pl.semaphore_signal(barrier, inc=1, device_id=plane_peer(k), device_id_type=MESH)

    w = weight_t[...].astype(F32)
    w = jnp.concatenate([w, jnp.zeros((C, 96), F32)], 1).T[0 : 9 * C]

    def tap(a, c):
        start = (3 * a + c) * C
        return w[start : start + C]

    def band(a, cells_in, shift, mirror=False):
        rows_iota = lax.broadcasted_iota(jnp.int32, (256, cells_in * C), 0) // C
        lanes_iota = lax.broadcasted_iota(jnp.int32, (256, cells_in * C), 1) // C - shift
        which = rows_iota - lanes_iota + 1
        if mirror:
            which = 2 - which
        out = jnp.zeros((256, cells_in * C), F32)
        for c in range(3):
            wide = jnp.concatenate([tap(a, c)] * 4, 1)
            wide = jnp.concatenate([wide] * (cells_in // 4), 1)
            out = jnp.where(which == c, jnp.concatenate([wide] * 8, 0), out)
        return out.astype(BF)

    slot_i = lax.broadcasted_iota(jnp.int32, (SL, T * T), 0)
    flat = jnp.where((mask_in[...] != 0) & (slot_i < count[0]), area_in[...], 0.0)
    flat = jnp.concatenate([flat, jnp.zeros((2, T * T), F32)], 0)
    for i in range(T):
        by_row[i] = jnp.concatenate([flat[:, T * i : T * i + T], jnp.zeros((8, 128 - T), F32)], 1)
    by_row[T:G] = jnp.zeros((G - T, 8, 128), F32)
    wa = [by_row[:, s, :] for s in range(SL)]
    hi, lo = split_hi_lo(jnp.concatenate(wa, 0))
    area_ref[...] = jnp.concatenate([hi, lo], 1)

    for m in range(NB):
        r_i = lax.broadcasted_iota(jnp.int32, (256, 256), 0)
        l_i = lax.broadcasted_iota(jnp.int32, (256, 256), 1)
        hit = (r_i & 127) == (l_i >> 5) + 8 * m
        spread[:, 256 * m : 256 * m + 256] = jnp.where(hit & ((r_i & 127) < T), 1.0, 0.0).astype(BF)

    for a in range(3):
        bands[a] = band(a, 8, 0)
    z32 = jnp.zeros((C, C), F32)
    z64 = jnp.zeros((C, 192), F32)
    wq_rows = []
    for a in range(3):
        wq_rows.append(jnp.concatenate([tap(a, 0), z32, z64], 1))
        wq_rows.append(jnp.concatenate([z64, z32, tap(a, 2)], 1))
    wq[...] = jnp.concatenate(wq_rows + [jnp.zeros((64, 256), F32)], 0).astype(BF)
    gl = jnp.concatenate([v for a in range(3) for v in (tap(2 - a, 2), z32)] + [z32, z32], 1)
    gr = jnp.concatenate([v for a in range(3) for v in (z32, tap(2 - a, 0))] + [z32, z32], 1)
    wqb[...] = jnp.concatenate([gl, jnp.zeros((192, 256), F32), gr], 0).astype(BF)

    @pl.when(t >= 0)
    def _():
        for copy in copies:
            copy.wait()
        wa = [by_row[:, s, :] for s in range(SL)]
        for side, row in ((0, 0), (1, T - 1)):
            lhs = [by_row[row, s : s + 1, :] for s in range(SL)] + [jnp.zeros((2, 128), F32)]
            lhs = jnp.concatenate(split_hi_lo(jnp.concatenate(lhs, 0)), 1)
            wide = dot(lhs, spread[...])
            for place, ref in ((0, xs), (8, gs)):
                v = [ref[s, row : row + 1, :].astype(F32) for s in range(SL)]
                v = jnp.concatenate(v + [jnp.zeros((2, W), F32)], 0)
                v = jnp.concatenate([v, jnp.zeros((8, WP - W), F32)], 1)
                v = v * wide if place else v
                v = jnp.where(wide > 0, v, 0.0)
                if place == 0:
                    kept = v
                else:
                    row_out[side] = jnp.concatenate([kept, v], 0).astype(BF)
        pad = jnp.zeros((G - T, 128), BF)
        for side, col in ((0, 0), (1, T - 1)):
            for s in range(SL):
                e = jnp.broadcast_to(wa[s][0:T, col : col + 1], (T, C))
                xv = jnp.where(e > 0, xs[s, :, C * col : C * col + C].astype(F32), 0.0)
                gv = jnp.where(e > 0, e * gs[s, :, C * col : C * col + C].astype(F32), 0.0)
                v = jnp.concatenate([xv, gv, jnp.zeros((T, 64), F32)], 1).astype(BF)
                col_out[side, s * G : (s + 1) * G] = jnp.concatenate([v, pad], 0)

    pl.semaphore_wait(barrier, n_tile + n_plane - 2)
    halo = []
    for src, dst, k, target in (
        (row_out.at[1], row_in.at[0], 0, tile_peer(n_tile - 1)),
        (row_out.at[0], row_in.at[1], 1, tile_peer(1)),
        (col_out.at[0], col_in.at[0], 2, face_peer(n_face - 1)),
        (col_out.at[1], col_in.at[1], 3, face_peer(1)),
    ):
        copy = pltpu.make_async_remote_copy(
            src_ref=src,
            dst_ref=dst,
            send_sem=halo_s.at[k],
            recv_sem=halo_r.at[k],
            device_id=target,
            device_id_type=MESH,
        )
        copy.start()
        halo.append(copy)

    def fetch(ref, m, lanes):
        parts = []
        for s in range(SL):
            start = 256 * m if isinstance(m, int) else pl.multiple_of(256 * m, 256)
            v = ref[s, :, pl.ds(start, lanes)].astype(F32)
            if lanes < 256:
                v = jnp.concatenate([v, jnp.zeros((T, 256 - lanes), F32)], 1)
            parts.append(v)
            parts.append(jnp.zeros((G - T, 256), F32))
        return jnp.concatenate(parts, 0)

    def down(v):
        return jnp.concatenate([v[R - 1 :], v[: R - 1]], 0)

    def up(v):
        return jnp.concatenate([v[1:], v[:1]], 0)

    def at(base, size, unit=128):
        return pl.ds(base if isinstance(base, int) else pl.multiple_of(base, unit), size)

    def blocks(body):
        for m in range(NB):
            body(m, 256 if m < NB - 1 else LAST)

    x1 = x3.at[1]
    @pl.when(t >= 0)
    def _():
        zcol = jnp.zeros((R, 128), BF)
        for a in range(3):
            s3[a, :, 0:128] = zcol
            s3[a, :, XW - 128 : XW] = zcol
        x1[:, XW - 128 : XW] = zcol
        gacc[0:8] = jnp.zeros((8, 256), F32)

        def prepare(m, lanes):
            e = dot(area_ref[...], spread[:, at(256 * m, 256)])
            blk = at(256 * m + 128, 256)
            wet[:, at(256 * m, 256)] = (e > 0).astype(F32).astype(BF)
            x1[:, blk] = jnp.where(e > 0, fetch(xs, m, lanes), 0.0).astype(BF)
            sv = jnp.where(e > 0, e * fetch(gs, m, lanes), 0.0).astype(BF)
            s3[0, :, blk] = down(sv)
            s3[1, :, blk] = sv
            s3[2, :, blk] = up(sv)
            gacc[0:8] = gacc[0:8] + jnp.sum(sv.astype(F32).reshape(R // 8, 8, 256), 0)

        blocks(prepare)
        row = jnp.sum(gacc[0:8], 0, keepdims=True)
        row = row[:, 0:128] + row[:, 128:256]
        row = row[:, 0:64] + row[:, 64:128]
        row = row[:, 0:C] + row[:, C : 2 * C]
        low = jnp.concatenate([row, jnp.zeros((1, 96), F32)], 1)
        part[96:128] = jnp.concatenate([low, jnp.zeros((31, 128), F32)], 0)

    for copy in halo:
        copy.wait()

    r_i = lax.broadcasted_iota(jnp.int32, (256, 128), 0)
    l_i = lax.broadcasted_iota(jnp.int32, (256, 128), 1)
    flip_l = jnp.where(r_i == 160 - 32 * (l_i >> 5) + (l_i & 31), 1.0, 0.0).astype(BF)
    r_i = lax.broadcasted_iota(jnp.int32, (G, G), 0)
    l_i = lax.broadcasted_iota(jnp.int32, (G, G), 1)
    flip_r = jnp.where(r_i + l_i == T - 1, 1.0, 0.0).astype(BF)
    zr = jnp.concatenate([row_in[0], row_in[1]], 0)
    zpad = jnp.concatenate([jnp.zeros((32, 128), BF), zr], 1)
    stacked = jnp.concatenate([zpad[:, 128 * (22 - n) : 128 * (24 - n)] for n in range(23)], 0)
    turned = dot(stacked, flip_l).astype(BF)
    flipped = jnp.concatenate(
        [turned[32 * n : 32 * n + 32] for n in range(23)] + [jnp.zeros((32, 128), BF)], 1
    )
    lane_i = lax.broadcasted_iota(jnp.int32, (128, 64), 1)
    row_i = lax.broadcasted_iota(jnp.int32, (128, 64), 0)
    sel = jnp.zeros((128, 64), F32)
    for s in range(SL):
        for side, halo_row in ((0, (16 * (s - 1) + 15) % 96), (1, 16 * s + 10)):
            n, r = nb[side, s], rev[side, s]
            src = 16 * side + 32 * r + lax.rem(jnp.maximum(n, 0), SL)
            src = jnp.where(n >= 0, src, -100)
            sel = jnp.where((row_i == halo_row) & (lane_i == src), 1.0, sel)
            rim_row = 96 + 16 * side + 8 * r + s
            sel = jnp.where((row_i == rim_row) & (lane_i == src + 8), 1.0, sel)
    routed = dot(sel.astype(BF), jnp.concatenate([zr, flipped], 0))
    for s in range(SL):
        rows = slice(G * s + 80, G * s + 96)
        old = x1[rows, 128 : 128 + WP].astype(F32)
        x1[rows, 128 : 128 + WP] = (old + routed[16 * s : 16 * s + 16]).astype(BF)
    hs = routed[96:128]
    hs_ref[...] = jnp.concatenate([jnp.zeros((32, 128), F32), hs, jnp.zeros((32, 128), F32)], 1)

    for side in range(2):
        flat = jnp.concatenate([col_in[side, s * G : (s + 1) * G] for s in range(SL)], 1)
        back = dot(flip_r, flat)
        for s in range(SL):
            cols[side, 0, s] = col_in[side, s * G : (s + 1) * G].astype(F32)
            cols[side, 1, s] = back[:, 128 * s : 128 * s + 128]
    ecol, xleft, xright = [], [], []
    for s in range(SL):
        got = []
        pieces = []
        for side in range(2):
            n, r = nb[2 + side, s], rev[2 + side, s]
            v = cols[side, r, lax.rem(jnp.maximum(n, 0), SL)]
            v = jnp.where(n >= 0, v, 0.0)
            got.append(v)
            pieces.append(jnp.where(r == 0, v, 0.0)[:, C : 2 * C])
            pieces.append(jnp.where(r == 1, v, 0.0)[:, C : 2 * C])
        ecol.append(jnp.concatenate(pieces, 1))
        xright.append(got[0][:, 0:C])
        xleft.append(got[1][:, 0:C])
    rim_col[...] = jnp.concatenate(ecol, 0)
    xright = jnp.concatenate(xright, 0)
    xleft = jnp.concatenate(xleft, 0)
    zc = jnp.zeros((R, C), F32)
    x1[:, 0:128] = jnp.concatenate([zc, zc, zc, xleft], 1).astype(BF)
    right = at(128 + 128 * 22, 128)
    x1[:, right] = (
        x1[:, right].astype(F32) + jnp.concatenate([zc, zc, xright, zc], 1)
    ).astype(BF)

    def move(n):
        left = x1[:, at(128 * n, 128)][:, 96:128]
        xp[:, at(128 * n, 128)] = jnp.concatenate(
            [left, x1[:, at(128 * n + 128, 128)][:, 0:96]], 1
        )

    for n in range(24):
        move(n)

    gacc[...] = jnp.zeros_like(gacc)

    def outer(m):
        sv = jnp.concatenate([s3[2 - a, :, at(128 * m + 128, 128)] for a in range(3)], 1)
        gacc[...] += lax.dot_general(
            sv, xp[:, at(128 * m, 256)], (((0,), (0,)), ((), ())), preferred_element_type=F32
        )

    for m in range(23):
        outer(m)
    grad = gacc[...]
    for a in range(3):
        total = None
        for j in range(4):
            piece = grad[128 * a + C * j : 128 * a + C * j + C, C * j : C * j + 96]
            total = piece if total is None else total + piece
        part[C * a : C * a + C] = jnp.concatenate([total, jnp.zeros((C, C), F32)], 1)

    def rows8(i):
        return pl.ds(pl.multiple_of(i * 8, 8), 8)

    sends = []
    for k in range(1, n_tile):
        copy = pltpu.make_async_remote_copy(
            src_ref=part.at[rows8(lax.rem(t + k, n_tile))],
            dst_ref=got1.at[k],
            send_sem=s_sem1.at[k],
            recv_sem=r_sem1.at[k],
            device_id=tile_peer(k),
            device_id_type=MESH,
        )
        copy.start()
        sends.append(copy)

    def beside(ref, m):
        mid = ref[:, at(256 * m, 128)][:, 96:128]
        far = ref[:, at(256 * m + 384, 128)][:, 0:C]
        q = jnp.concatenate([mid, far, mid, far], 1)
        lane = lax.broadcasted_iota(jnp.int32, (R, 128), 1)
        return jnp.concatenate([jnp.where(lane < 64, down(q), q), up(q)], 1)

    bias_row = jnp.concatenate([bias[...]] * 8, 1)

    def forward(m, lanes):
        blk = at(256 * m + 128, 256)
        y = dot(x3[0, :, blk], bands[0]) + dot(x3[1, :, blk], bands[1])
        y = y + dot(x3[2, :, blk], bands[2]) + dot(beside(x1, m), wq[...]) + bias_row
        y = (y * wet[:, at(256 * m, 256)].astype(F32)).astype(BF)
        for s in range(SL):
            xs[s, :, at(256 * m, lanes)] = y[G * s : G * s + T, :lanes]

    @pl.when(t >= 0)
    def _():
        for side, a in ((0, 2), (1, 0)):
            total = None
            for r in range(2):
                rows = hs_ref[16 * side + 8 * r : 16 * side + 8 * r + 8]
                lhs = jnp.concatenate(
                    [rows[:, 256 * m : 256 * m + 512] for m in range(NB)], 0
                ).astype(BF)
                part_sum = dot_t(lhs, band(a, 16, 4, mirror=(r == 1)))
                total = part_sum if total is None else total + part_sum
            rim[side] = total.astype(BF).astype(F32)
        ecol = rim_col[...]
        z32 = jnp.zeros((C, C), F32)
        e3 = jnp.concatenate(
            [pltpu.roll(ecol, 1, 0), ecol, pltpu.roll(ecol, R - 1, 0)], 1
        ).astype(BF)
        v2 = jnp.concatenate(
            [v for a in range(3) for v in (tap(2 - a, 0), tap(a, 0), z32, z32)], 1
        )
        v3 = jnp.concatenate(
            [v for a in range(3) for v in (z32, z32, tap(2 - a, 2), tap(a, 2))], 1
        )
        rc = dot_t(e3, jnp.concatenate([v2, v3], 0).astype(BF)).astype(BF).astype(F32)
        rim_col[...] = jnp.concatenate([rc, jnp.zeros((R, 64), F32)], 1)
        for n in range(24):
            xv = x1[:, at(128 * n + 128, 128)]
            x3[0, :, at(128 * n + 128, 128)] = down(xv)
            x3[2, :, at(128 * n + 128, 128)] = up(xv)
        for m in range(5):
            forward(m, 256)

    for copy in sends:
        copy.wait()
    total = part[rows8(t)]
    for k in range(1, n_tile):
        total = total + got1[k]
    mine[...] = total
    sends = []
    for k in range(1, n_plane):
        copy = pltpu.make_async_remote_copy(
            src_ref=mine,
            dst_ref=got2.at[me],
            send_sem=s_sem2.at[k],
            recv_sem=r_sem2.at[k],
            device_id=plane_peer(k),
            device_id_type=MESH,
        )
        copy.start()
        sends.append(copy)
    got2[me] = total

    @pl.when(t >= 0)
    def _():
        for m in range(5, NB):
            forward(m, 256 if m < NB - 1 else LAST)

    out_copies = []
    for s in range(SL):
        out_copies.append(pltpu.make_async_copy(xs.at[s], y_hbm.at[0, s], out_sem.at[0, s]))
        out_copies[-1].start()

    row8 = lax.broadcasted_iota(jnp.int32, (8, 256), 0)
    z6 = jnp.zeros((R, 192), F32)
    zc = jnp.zeros((R, C), F32)

    def backward(m, lanes):
        blk = at(256 * m + 128, 256)
        y = dot_t(s3[0, :, blk], bands[2]) + dot_t(s3[1, :, blk], bands[1])
        y = y + dot_t(s3[2, :, blk], bands[0]) + dot_t(beside(s3.at[1], m), wqb[...])
        if isinstance(m, int) and m == 0:
            y = y + jnp.concatenate([rim_col[:, C : 2 * C], zc, z6], 1)
        if isinstance(m, int) and m == NB - 1:
            y = y + jnp.concatenate([zc, rim_col[:, 0:C], z6], 1)
        parts = []
        tops = rim[0, at(8 * m, 8, 8), :]
        lows = rim[1, at(8 * m, 8, 8), :]
        for s in range(SL):
            parts.append(y[G * s : G * s + 8] + jnp.where(row8 == 0, tops[s : s + 1], 0.0))
            parts.append(y[G * s + 8 : G * s + 88])
            parts.append(y[G * s + 88 : G * s + 96] + jnp.where(row8 == 1, lows[s : s + 1], 0.0))
        y = jnp.concatenate(parts, 0)
        y = (y * wet[:, at(256 * m, 256)].astype(F32)).astype(BF)
        for s in range(SL):
            gs[s, :, at(256 * m, lanes)] = y[G * s : G * s + T, :lanes]

    for copy in sends:
        copy.wait()
    total = got2[0]
    for k in range(1, n_plane):
        total = total + got2[k]
    full[rows8(t)] = total * scale
    sends = []
    for k in range(1, n_tile):
        copy = pltpu.make_async_remote_copy(
            src_ref=full.at[rows8(t)],
            dst_ref=full.at[rows8(t)],
            send_sem=s_sem3.at[k],
            recv_sem=r_sem3.at[k],
            device_id=tile_peer(k),
            device_id_type=MESH,
        )
        copy.start()
        sends.append(copy)

    @pl.when(t >= 0)
    def _():
        for m in range(NB):
            backward(m, 256 if m < NB - 1 else LAST)

    for s in range(SL):
        out_copies.append(pltpu.make_async_copy(gs.at[s], gi_hbm.at[0, s], out_sem.at[1, s]))
        out_copies[-1].start()

    for copy in sends:
        copy.wait()
    w_out[...] = jnp.concatenate([full[C * a : C * a + C, 0 : 3 * C] for a in range(3)], 1)
    b_out[...] = full[96:97, 0:C]
    for copy in out_copies:
        copy.wait()


def settle_kernel(y_in, gi_in, w_in, b_in, y, gi, w, b, ys, gis, in_sem, out_sem):
    pairs = ((y_in, ys, y), (gi_in, gis, gi))
    loads = [
        pltpu.make_async_copy(src.at[0, s], mid.at[s], in_sem.at[i, s])
        for s in range(SL)
        for i, (src, mid, dst) in enumerate(pairs)
    ]
    stores = [
        pltpu.make_async_copy(mid.at[s], dst.at[0, s], out_sem.at[i, s])
        for s in range(SL)
        for i, (src, mid, dst) in enumerate(pairs)
    ]
    for load in loads:
        load.start()
    w[...] = w_in[...]
    b[...] = b_in[...]
    for load, store in zip(loads, stores):
        load.wait()
        store.start()
    for store in stores:
        store.wait()


def settle(y, gi, w, b):
    any_ = pl.BlockSpec(memory_space=pl.ANY)
    vm = pl.BlockSpec(memory_space=pltpu.VMEM)
    return pl.pallas_call(
        settle_kernel,
        in_specs=[any_, any_, vm, vm],
        out_specs=[any_, any_, vm, vm],
        out_shape=[jax.ShapeDtypeStruct(v.shape, v.dtype) for v in (y, gi, w, b)],
        scratch_shapes=[
            pltpu.VMEM((SL, T, W), BF),
            pltpu.VMEM((SL, T, W), BF),
            pltpu.SemaphoreType.DMA((2, SL)),
            pltpu.SemaphoreType.DMA((2, SL)),
        ],
        compiler_params=pltpu.CompilerParams(vmem_limit_bytes=VMEM_LIMIT),
    )(y, gi, w, b)


def per_device(
    inputs, cotangent, conv_weight, out_bias, cell_area, land_mask, neighbours, reversal, wet_count
):
    n_face, n_tile, n_dp = (lax.axis_size(a) for a in ("face", "tile", "dp"))
    n_plane = n_face * n_dp
    scale = 1.0 / math.sqrt(n_dp * n_face * n_tile * SL * T * T)
    any_ = pl.BlockSpec(memory_space=pl.ANY)
    vm = pl.BlockSpec(memory_space=pltpu.VMEM)
    sm = pl.BlockSpec(memory_space=pltpu.SMEM)
    tiles = jax.ShapeDtypeStruct((1, SL, T, W), BF)
    dma = pltpu.SemaphoreType.DMA
    outputs, input_grad, w_sum, b_sum = pl.pallas_call(
        functools.partial(device_kernel, (n_face, n_tile, n_dp, scale)),
        in_specs=[sm, sm, any_, any_, sm] + [vm] * 4,
        out_specs=[any_, any_, vm, vm],
        out_shape=[
            tiles,
            tiles,
            jax.ShapeDtypeStruct((C, 9 * C), F32),
            jax.ShapeDtypeStruct((1, C), F32),
        ],
        scratch_shapes=[
            pltpu.VMEM((SL, T, W), BF),
            pltpu.VMEM((SL, T, W), BF),
            pltpu.VMEM((256, WP), BF),
            pltpu.VMEM((G, 8, 128), F32),
            pltpu.VMEM((R, 256), BF),
            pltpu.VMEM((3, 256, 256), BF),
            pltpu.VMEM((256, 256), BF),
            pltpu.VMEM((256, 256), BF),
            pltpu.VMEM((R, 128), F32),
            pltpu.VMEM((32, XW), F32),
            pltpu.VMEM((3, R, XW), BF),
            pltpu.VMEM((3, R, XW), BF),
            pltpu.VMEM((R, WP), BF),
            pltpu.VMEM((R, WP), BF),
            pltpu.VMEM((2, 2, SL, G, 128), F32),
            pltpu.VMEM((2, 16, WP), BF),
            pltpu.VMEM((2, 16, WP), BF),
            pltpu.VMEM((2, R, 128), BF),
            pltpu.VMEM((2, R, 128), BF),
            pltpu.VMEM((2, 8 * NB, 256), F32),
            pltpu.VMEM((384, 256), F32),
            pltpu.VMEM((128, 128), F32),
            pltpu.VMEM((n_tile, 8, 128), F32),
            pltpu.VMEM((8, 128), F32),
            pltpu.VMEM((n_plane, 8, 128), F32),
            pltpu.VMEM((128, 128), F32),
            dma((2, SL)),
            dma((2, SL)),
            dma((4,)),
            dma((4,)),
            dma((n_tile,)),
            dma((n_tile,)),
            dma((n_plane,)),
            dma((n_plane,)),
            dma((n_tile,)),
            dma((n_tile,)),
        ],
        compiler_params=pltpu.CompilerParams(
            vmem_limit_bytes=VMEM_LIMIT, collective_id=0, has_side_effects=True
        ),
    )(
        neighbours.T,
        reversal.T,
        inputs,
        cotangent,
        wet_count,
        cell_area,
        land_mask,
        conv_weight.T,
        out_bias[None],
    )
    outputs, input_grad, w_sum, b_sum = settle(outputs, input_grad, w_sum, b_sum)
    return outputs, input_grad, w_sum.T, b_sum[0]


def solution(mesh):
    return jax.shard_map(
        per_device,
        mesh=mesh,
        in_specs=(
            P("dp", ("face", "tile"), None, None),
            P("dp", ("face", "tile"), None, None),
            P(),
            P(),
            P(("face", "tile"), None),
            P(("face", "tile"), None),
            P(("face", "tile"), None),
            P(("face", "tile"), None),
            P(("face", "tile")),
        ),
        out_specs=(
            P("dp", ("face", "tile"), None, None),
            P("dp", ("face", "tile"), None, None),
            P(),
            P(),
        ),
        check_vma=False,
    )
```
